128 devices in a mesh: row: 8 (over x, core), col: 16 (over y, z).
Axes of the slice: x: 4, y: 4, z: 4, core: 2. Of those that a mesh axis runs over, the one named last changes fastest.
Arguments:
- integrals: bfloat16 [8, 3, 32, 32, 6400], P('row', None, None, None, 'col'), may hold values from -2.5 to 2.5
- block_sizes: int32 [8], replicated, may hold values from 8 to 32, as said below
- int_pattern: int32 [8, 3, 64], replicated, may hold values 0 or 1
- occ_density: bfloat16 [8, 3, 32, 32], replicated, may hold values from -0.625 to 0.625
- occ_pattern: int32 [8, 3], replicated, may hold values 0 or 1
- vir_density: bfloat16 [8, 3, 32, 32], replicated, may hold values from -0.625 to 0.625
- vir_pattern: int32 [8, 3], replicated, may hold values 0 or 1
Outputs:
- response: float32 [6400, 6400], P('row', 'col')
The draws below stay inside these ranges and needn't reach their ends.
Inputs may be any that keep to these rules, and one draw needn't show every extreme that they name: `block_sizes`: every atom block holds at least 8 functions, and some block holds exactly 32.
All inputs are finite; a program needn't handle non-finite values.
Results may differ from the reference program's by a relative error of at most 0.015.
Values may be sent and summed in bfloat16 or wider, within the bound.
A program may use at most 128 MiB of HBM per device.

```python
import jax
import jax.numpy as jnp
from jax import lax

BLK = 32
ND = 3
PB = 100
NP = 6400
NB = 8
N_ROW = 8
N_COL = 16


def draw_block_sizes(key, part):
    key = jax.random.fold_in(key, 11)
    size_key, spot_key = jax.random.split(key)
    drawn = jax.random.randint(size_key, (NB,), BLK // 4, BLK + 1)
    spot_index = jax.random.randint(spot_key, (), 0, NB)
    return jnp.where(jnp.arange(NB) == spot_index, BLK, drawn).astype(jnp.int32)


def plant(result, stream_key, least, top_value):
    place = [jax.random.randint(jax.random.fold_in(stream_key, axis), (), 0, length) for axis, length in enumerate(result.shape)]
    longest = result.shape.index(max(result.shape))
    neighbour = place[:longest] + [(place[longest] + 1) % result.shape[longest]] + place[longest + 1:]
    return result.at[tuple(place)].set(least).at[tuple(neighbour)].set(top_value)


def block_scale(stream_key, dims, shards, least, top_value):
    level, own = 1.0, jax.random.fold_in(stream_key, 6)
    for position, blocks in shards:
        heights = jnp.exp(jax.random.uniform(jax.random.fold_in(own, position), (blocks,), jnp.float32, least / len(shards), top_value / len(shards)))
        level = level * jnp.repeat(heights, dims[position] // blocks).reshape([-1 if axis == position else 1 for axis in range(len(dims))])
    return level


def normal_values(stream_key, shape, spread, bound, cuts=(), kind=jnp.bfloat16):
    entries = spread * jax.random.normal(stream_key, shape, jnp.float32)
    if cuts:
        entries = entries * block_scale(stream_key, shape, cuts, -0.22, 0.18)
    return jnp.clip(entries, -bound, bound).astype(kind)


def setup_inputs(seed: int = 0) -> dict:
    streams_of = jax.random.split(jax.random.key(seed), 8)
    integrals = normal_values(streams_of[0], (NB, ND, BLK, BLK, NP), 0.16, 2.5, ((0, 8), (4, 16)))
    block_sizes = draw_block_sizes(jax.random.fold_in(streams_of[7], 71), 0)
    int_pattern = plant((jax.random.randint(streams_of[2], (NB, ND, NP // PB), 0, 4) < 3).astype(jnp.int32), jax.random.fold_in(streams_of[2], 1), 0, 1)
    occ_density = normal_values(streams_of[3], (NB, ND, BLK, BLK), (ND * BLK) ** -0.5, 0.625)
    occ_pattern = plant((jax.random.randint(streams_of[4], (NB, ND), 0, 5) < 4).astype(jnp.int32), jax.random.fold_in(streams_of[4], 1), 0, 1)
    vir_density = normal_values(streams_of[5], (NB, ND, BLK, BLK), (ND * BLK) ** -0.5, 0.625)
    vir_pattern = plant((jax.random.randint(streams_of[6], (NB, ND), 0, 5) < 4).astype(jnp.int32), jax.random.fold_in(streams_of[6], 1), 0, 1)
    return dict(integrals=integrals, block_sizes=block_sizes, int_pattern=int_pattern, occ_density=occ_density, occ_pattern=occ_pattern, vir_density=vir_density, vir_pattern=vir_pattern)


def slot_masks(block_sizes):
    slot_ids = jnp.arange(BLK, dtype=jnp.int32)
    return (slot_ids[None, :] < block_sizes[:, None]).astype(jnp.bfloat16)


def function_order():
    sub_width = NP // (N_ROW * N_COL)
    return jnp.arange(NP, dtype=jnp.int32).reshape(N_COL, N_ROW, sub_width).transpose(1, 0, 2).reshape(NP)


def reference(integrals, block_sizes, int_pattern, occ_density, occ_pattern, vir_density, vir_pattern):
    slot_fill = slot_masks(block_sizes)
    blocks = jnp.arange(NB, dtype=jnp.int32)
    ri_order = function_order()
    ri_fill = jnp.repeat(int_pattern.astype(jnp.bfloat16), PB, axis=2)[:, :, ri_order]
    ints_sorted = integrals[..., ri_order]
    pieces = []
    for band_off in range(ND):
        partner = (blocks + band_off - 1) % NB
        pieces.append(ints_sorted[:, band_off] * slot_fill[:, :, None, None] * slot_fill[partner][:, None, :, None] * ri_fill[:, band_off][:, None, None, :])
    live_ints = jnp.stack(pieces, axis=1)
    occupied = occ_density * occ_pattern.astype(jnp.bfloat16)[:, :, None, None]
    virtual = vir_density * vir_pattern.astype(jnp.bfloat16)[:, :, None, None]
    mixed_list = []
    for out_band in range(ND):
        summed = jnp.zeros((NB, BLK, BLK, NP), jnp.float32)
        for mid_band in range(ND):
            step_band = out_band - mid_band + 1
            if 0 <= step_band < ND:
                density = occupied[(blocks + mid_band - 1) % NB, step_band].astype(jnp.float32)
                summed = summed + jnp.einsum('iabp,ibc->iacp', live_ints[:, mid_band].astype(jnp.float32), density)
        mixed_list.append(summed.astype(jnp.bfloat16))
    mixed_blocks = jnp.stack(mixed_list, axis=1)
    contracted_list = []
    for out_band in range(ND):
        summed = jnp.zeros((NB, BLK, BLK, NP), jnp.float32)
        for shift_band in range(ND):
            mid_band = out_band - shift_band + 1
            if 0 <= mid_band < ND:
                source = mixed_blocks[(blocks + shift_band - 1) % NB, mid_band].astype(jnp.float32)
                summed = summed + jnp.einsum('ixa,iacp->ixcp', virtual[:, shift_band].astype(jnp.float32), source)
        contracted_list.append(summed.astype(jnp.bfloat16))
    contracted = jnp.stack(contracted_list, axis=1)
    group_rows = NB * ND * BLK * BLK // N_COL
    left_rows = contracted.reshape(N_COL, group_rows, NP)
    right_rows = live_ints.reshape(N_COL, group_rows, NP)

    def add_group(running, pair_rows):
        product = jnp.dot(pair_rows[0].astype(jnp.float32).T, pair_rows[1].astype(jnp.float32), preferred_element_type=jnp.float32, precision=lax.Precision.HIGHEST)
        rounded = lax.optimization_barrier(product.astype(jnp.bfloat16))
        return running + rounded.astype(jnp.float32), None

    response, _ = lax.scan(add_group, jnp.zeros((NP, NP), jnp.float32), (left_rows, right_rows))
    return response
```

```python
import jax
import jax.numpy as jnp
from jax import lax
from jax.experimental import pallas as pl
from jax.experimental.pallas import tpu as pltpu
from jax.sharding import PartitionSpec as P

BLK = 32
ND = 3
PB = 100
NB = 8
NX = 4
W = 400
SUB = 50
SLOT = 64
PIECE = 512
NPIECE = 6
LANES = 256
QOFF = (0, 400, 800, 1280)
QROWS = 1792
MESH = pl.DeviceIdType.MESH
NT = (((1,), (1,)), ((), ()))
NN = (((1,), (0,)), ((), ()))
GROUPS = (
    ((0,), 0, 1280, (0, 1, 2)),
    ((1, 2), 0, 1280, (0, 1, 2)),
    ((0, 1, 2), 1280, 512, (3,)),
    ((3,), 0, 1792, (0, 1, 2, 3)),
)


def iota(shape, dim):
    return lax.broadcasted_iota(jnp.int32, shape, dim)


def dot(a, b, dims=NN):
    return lax.dot_general(a, b, dims, preferred_element_type=jnp.float32)


def wrap(v, n=NX):
    return lax.rem(v + n, n)


def kernel(
    sizes, ri, occ_pat, vir_pat, ints, occ, vir, out,
    right, left, mixed, halo, occ_mat, vir_mat, acc, fin, one_hot, msgs, got,
    s0, s1, s2, s3, d0, d1, d2, d3, x0, x1, x2, x3,
    r_send, r_recv, l_send, l_recv, h_send, h_recv, c_send, c_recv, x_send, x_recv, a_send, a_recv,
):
    parts, cores, hops = (s0, s1, s2, s3), (d0, d1, d2, d3), (x0, x1, x2, x3)
    row = lax.axis_index("row")
    col = lax.axis_index("col")
    x, k = row // 2, lax.rem(row, 2)
    y, z = col // NX, lax.rem(col, NX)
    bf = jnp.bfloat16

    def at(nx, nk, ny, nz):
        return (2 * nx + nk, NX * ny + nz)

    up_x, down_x, far_x = wrap(x + 1), wrap(x - 1), wrap(x + 2)
    y_dev = (at(x, k, wrap(y + 1), z), at(x, k, wrap(y - 1), z))
    z_dev = (at(x, k, y, wrap(z + 1)), at(x, k, y, wrap(z - 1)))
    x_dev = (at(up_x, k, y, z), at(down_x, k, y, z))
    h_dev = ((wrap(row + 1, NB), col), (wrap(row - 1, NB), col))
    other = at(x, 1 - k, y, z)
    far_halo = (wrap(row + 2 * k - 1, NB), col)

    barrier = pltpu.get_barrier_semaphore()
    for target in (x_dev[0], x_dev[1], other, far_halo):
        pl.semaphore_signal(barrier, inc=1, device_id=target, device_id_type=MESH)

    def greet(n, _):
        target = (row, NX * wrap(y + n // NX) + wrap(z + lax.rem(n, NX)))
        pl.semaphore_signal(barrier, inc=1, device_id=target, device_id_type=MESH)
        return 0

    lax.fori_loop(1, NX * NX, greet, 0)

    def remote(src, dst, send, recv, target):
        return pltpu.make_async_remote_copy(
            src_ref=src, dst_ref=dst, send_sem=send, recv_sem=recv, device_id=target, device_id_type=MESH
        )

    own_size = sizes[row]
    eye = iota((W, W), 0) == iota((W, W), 1)
    ri_block = iota((1, W), 1) // PB

    def turn(p, _):
        e = p // 2
        keep = jnp.zeros((1, W), jnp.float32)
        for q in range(W // PB):
            value = ri[row, e, NX * col + q].astype(jnp.float32)
            keep = jnp.where(ri_block == q, value, keep)
        diag = jnp.where(eye, keep, 0.0).astype(bf)
        lane = iota((1, PIECE), 1) + lax.rem(p, 2) * PIECE
        partner = sizes[wrap(row + e - 1, NB)]
        fill = jnp.where((lane // BLK < own_size) & (lane % BLK < partner), 1.0, 0.0)
        rows = ints[e, pl.ds(pl.multiple_of(lax.rem(p, 2) * PIECE, PIECE), PIECE), :]
        right[p, 0:W, :] = (dot(diag, rows, NT) * fill).astype(bf)
        return 0

    lax.fori_loop(0, NPIECE, turn, 0)
    pl.semaphore_wait(barrier, NX * NX - 1 + 4)

    def gather_copies(view, send, recv, targets):
        own, onward = {}, {}
        for way in (0, 1):
            for p in range(NPIECE):
                own[way, p] = remote(
                    view(p, 0), view(p, 1 + way), send.at[way, p], recv.at[way, p], targets[way]
                )
            for j in range(ND):
                p = 2 * j + way
                onward[way, j] = remote(
                    view(p, 1 + way), view(p, 3), send.at[way, NPIECE + j], recv.at[way, NPIECE + j], targets[way]
                )
        return own, onward

    def right_view(p, slot):
        return right.at[p, pl.ds(QOFF[slot], W), :]

    def left_view(p, slot):
        return left.at[p, slot]

    r_own, r_on = gather_copies(right_view, r_send, r_recv, y_dev)
    l_own, l_on = gather_copies(left_view, l_send, l_recv, z_dev)
    for p in range(NPIECE):
        for way in (0, 1):
            r_own[way, p].start()

    inner = (iota((LANES, BLK), 0) % BLK == iota((LANES, BLK), 1)).astype(bf)
    same = iota((LANES, LANES), 0) // BLK == iota((LANES, LANES), 1) // BLK

    def spread_occ(n, _):
        e, f = n // ND, lax.rem(n, ND)
        j = wrap(row + e - 1, NB)
        block = (occ[j, f].astype(jnp.float32) * occ_pat[j, f].astype(jnp.float32)).astype(bf)
        wide = dot(dot(inner, block).astype(bf), inner, NT)
        occ_mat[n] = jnp.where(same, wide, 0.0).astype(bf)
        return 0

    lax.fori_loop(0, ND * ND, spread_occ, 0)

    halos = {}
    for way, order in ((0, (1, 2)), (1, (1, 0))):
        for j, band in enumerate(order):
            halos[way, j] = remote(
                mixed.at[band], halo.at[2 * way + j], h_send.at[way, j], h_recv.at[way, j], h_dev[way]
            )

    def mix(dm):
        def body(g, _):
            h, start = g // 2, pl.multiple_of(lax.rem(g, 2) * LANES, LANES)
            total = None
            for e in range(ND):
                f = dm + 1 - e
                if 0 <= f < ND:
                    term = dot(right[2 * e + h, 0:W, pl.ds(start, LANES)], occ_mat[ND * e + f])
                    total = term if total is None else total + term
            mixed[dm, :, pl.ds(pl.multiple_of(g * LANES, LANES), LANES)] = total.astype(bf)
            return 0

        lax.fori_loop(0, BLK * BLK // LANES, body, 0)

    mix(1)
    halos[0, 0].start()
    halos[1, 0].start()
    mix(2)
    halos[0, 1].start()
    mix(0)
    halos[1, 1].start()

    def spread_vir(n, _):
        g, part = n // NX, lax.rem(n, NX)
        block = (vir[row, g].astype(jnp.float32) * vir_pat[row, g].astype(jnp.float32)).astype(bf)
        outer = (iota((BLK * BLK, BLK), 0) // BLK == iota((BLK * BLK, BLK), 1)).astype(bf)
        tall = dot(outer, block, NT).astype(bf)
        columns = iota((LANES, BLK), 0) + part * LANES
        wide = dot(tall, (columns // BLK == iota((LANES, BLK), 1)).astype(bf), NT)
        match = iota((BLK * BLK, LANES), 0) % BLK == iota((BLK * BLK, LANES), 1) % BLK
        vir_mat[g, :, pl.ds(pl.multiple_of(part * LANES, LANES), LANES)] = jnp.where(match, wide, 0.0).astype(bf)
        return 0

    lax.fori_loop(0, ND * NX, spread_vir, 0)

    def contract(d, terms):
        def body(h, _):
            columns = pl.ds(pl.multiple_of(h * PIECE, PIECE), PIECE)
            total = None
            for ref, index, g in terms:
                term = dot(ref[index], vir_mat[g, :, columns])
                total = term if total is None else total + term
            left[2 * d + h, 0] = total.astype(bf)
            return 0

        lax.fori_loop(0, 2, body, 0)
        for h in (0, 1):
            for way in (0, 1):
                l_own[way, 2 * d + h].start()

    halos[0, 0].wait_recv()
    contract(0, ((halo, 0, 0), (mixed, 0, 1)))
    halos[1, 0].wait_recv()
    contract(2, ((mixed, 2, 1), (halo, 2, 2)))
    halos[0, 1].wait_recv()
    halos[1, 1].wait_recv()
    contract(1, ((halo, 1, 0), (mixed, 1, 1), (halo, 3, 2)))
    l_order = (0, 1, 4, 5, 2, 3)

    for yy in (0, 1):
        source = iota((W, 8 * 128), 0)
        target = iota((W, 8 * 128), 1)
        hit = (source // SUB == target // 128) & (target % 128 == yy * SUB + source % SUB)
        one_hot[yy] = jnp.where(hit, 1.0, 0.0).astype(bf)
    for p in range(NPIECE):
        right[p, 1200:1280, :] = jnp.zeros((80, PIECE), bf)
        right[p, 1680:1792, :] = jnp.zeros((112, PIECE), bf)
    acc[W:, :] = jnp.zeros((acc.shape[0] - W, acc.shape[1]), jnp.float32)

    def product(slot, first, lanes, pieces=tuple(range(NPIECE)), add=False):
        def body(n, _):
            start = pl.multiple_of(n * LANES, LANES)
            q_rows = pl.ds(pl.multiple_of(first + n * LANES, LANES), LANES)
            total = acc[0:W, pl.ds(start, LANES)] if add else None
            for p in pieces:
                term = dot(left[p, slot], right[p, q_rows, :], NT)
                total = term if total is None else total + term
            acc[0:W, pl.ds(start, LANES)] = total
            return 0

        lax.fori_loop(0, lanes // LANES, body, 0)

    def split(n, which):
        lanes = GROUPS[n][2]
        for s in range(8):
            parts[n][s % 2, s // 2, which] = acc[SUB * s : SUB * s + SLOT, 0:lanes].astype(bf)

    core_copy, hop_copy = {}, {}

    def core_start(n):
        core_copy[n] = remote(parts[n].at[1 - k], cores[n], c_send.at[n], c_recv.at[n], other)
        core_copy[n].start()

    half = SLOT // 2
    low, high = pl.ds(0, half), pl.ds(half, half)

    def hop(n, way, m, src):
        hop_copy[n, way, m] = remote(
            src, hops[n].at[way, m], x_send.at[n, way, m], x_recv.at[n, way, m], x_dev[way]
        )
        hop_copy[n, way, m].start()

    def stage1(n):
        ref, extra = parts[n], cores[n]
        core_copy[n].wait_recv()
        mine = ref.at[k]

        def join(b):
            mine[b] = (mine[b].astype(jnp.float32) + extra[b].astype(jnp.float32)).astype(bf)

        join(far_x)
        hop(n, 0, 0, mine.at[far_x, :, low, :])
        hop(n, 1, 0, mine.at[far_x, :, high, :])
        join(up_x)
        hop(n, 0, 1, mine.at[up_x, :, high, :])
        join(down_x)
        hop(n, 1, 1, mine.at[down_x, :, low, :])
        join(x)

    def stage2(n):
        mine = parts[n].at[k]
        for way, b, rows in ((0, up_x, low), (1, down_x, high)):
            hop_copy[n, way, 0].wait_recv()
            mine[b, :, rows, :] = (
                mine[b, :, rows, :].astype(jnp.float32) + hops[n][way, 0].astype(jnp.float32)
            ).astype(bf)
            hop(n, way, 2, mine.at[b, :, rows, :])

    def stage3(n):
        slots, _, _, q_slots = GROUPS[n]
        mine = parts[n].at[k]
        for way in (0, 1):
            for m in (1, 2):
                hop_copy[n, way, m].wait_recv()
        for rows, one, two in ((low, 2, 1), (high, 1, 2)):
            total = (
                mine[x, :, rows, :].astype(jnp.float32)
                + hops[n][0, one].astype(jnp.float32)
                + hops[n][1, two].astype(jnp.float32)
            )
            for i, slot in enumerate(slots):
                for q in q_slots:
                    lane = QOFF[q] - GROUPS[n][1]
                    there = wrap(y + (0, -1, 1, 2)[q])
                    fin[slot, there, rows, :] = total[i, :, lane : lane + W].astype(bf)

    exchange = {}

    def exchange_start(n, slots):
        for slot in slots:
            for pair in (0, 1):
                packed = (dot(fin[slot, 2 * pair], one_hot[0]) + dot(fin[slot, 2 * pair + 1], one_hot[1])).astype(bf)
                for s in range(8):
                    target = NX * (s // 2) + 2 * (s % 2) + pair
                    msgs[target, slot] = packed[:, 128 * s : 128 * s + 128]
        which = pl.ds(slots[0], len(slots))

        def copy(m):
            target = NX * wrap(y + m // NX) + wrap(z + lax.rem(m, NX))
            return remote(
                msgs.at[target, which], got.at[col, which], a_send.at[n, m - 1], a_recv.at[n, m - 1], (row, target)
            )

        exchange[n] = copy

        def begin(m, _):
            copy(m).start()
            return 0

        lax.fori_loop(1, NX * NX, begin, 0)
        for slot in slots:
            got[col, slot] = msgs[col, slot]

    def exchange_wait(n, what):
        def body(m, _):
            if what == "recv":
                exchange[n](m).wait_recv()
            else:
                exchange[n](m).wait_send()
            return 0

        lax.fori_loop(1, NX * NX, body, 0)

    for p in range(NPIECE):
        for way in (0, 1):
            r_own[way, p].wait_recv()
            if p % 2 == way:
                r_on[way, p // 2].start()
    product(0, 0, 1280)
    split(0, 0)
    core_start(0)
    for p in l_order:
        for way in (0, 1):
            l_own[way, p].wait_recv()
            if p % 2 == way:
                l_on[way, p // 2].start()
    stage1(0)
    product(1, 0, 1280)
    split(1, 0)
    product(2, 0, 1280)
    split(1, 1)
    core_start(1)
    stage2(0)
    for j in range(ND):
        for way in (0, 1):
            r_on[way, j].wait_recv()
    stage1(1)
    stage3(0)
    for i, slot in enumerate((0, 1, 2)):
        product(slot, 1280, 512)
        split(2, i)
    core_start(2)
    stage2(1)
    steps = [lambda: stage1(2), lambda: stage3(1), lambda: stage2(2), lambda: stage3(2)]
    seen = 0
    for j in (0, 2, 1):
        for way in (0, 1):
            l_on[way, j].wait_recv()
            product(3, 0, 1792, (2 * j + way,), add=seen > 0)
            seen += 1
            if steps and seen >= 1 and seen <= 4:
                steps.pop(0)()
    split(3, 0)
    core_start(3)
    exchange_start(0, (0, 1, 2))
    stage1(3)
    stage2(3)
    stage3(3)
    exchange_start(1, (3,))

    source = iota((4 * 128, W), 0)
    target = iota((4 * 128, W), 1)
    inside = source % 128
    place = jnp.where(
        (inside < 2 * SUB) & (target == (4 * (inside // SUB) + source // 128) * SUB + inside % SUB), 1.0, 0.0
    ).astype(bf)
    exchange_wait(0, "recv")
    exchange_wait(1, "recv")
    slot_of = {0: 0, 3: 1, 1: 2, 2: 3}
    for yy in range(NX):
        for zz in range(NX):
            pieces = [got[NX * yy + src, slot_of[(zz - src) % NX]] for src in range(NX)]
            block = dot(jnp.concatenate(pieces, axis=1), place)
            start = (NX * yy + zz) * SUB
            out[start : start + SUB, :] = block[0:SUB]

    for copies in (r_own, r_on, l_own, l_on, halos, core_copy, hop_copy):
        for copy in copies.values():
            copy.wait_send()
    exchange_wait(0, "send")
    exchange_wait(1, "send")


def local(integrals, block_sizes, int_pattern, occ_density, occ_pattern, vir_density, vir_pattern):
    ints = integrals.reshape(ND, BLK * BLK, W)
    bf = jnp.bfloat16
    vmem = pl.BlockSpec(memory_space=pltpu.VMEM)
    smem = pl.BlockSpec(memory_space=pltpu.SMEM)
    dma = pltpu.SemaphoreType.DMA
    group_shapes = [(len(g[0]), g[2]) for g in GROUPS]
    scratch = [
        pltpu.VMEM((NPIECE, QROWS, PIECE), bf),
        pltpu.VMEM((NPIECE, NX, W, PIECE), bf),
        pltpu.VMEM((ND, W, BLK * BLK), bf),
        pltpu.VMEM((4, W, BLK * BLK), bf),
        pltpu.VMEM((ND * ND, LANES, LANES), bf),
        pltpu.VMEM((ND, BLK * BLK, BLK * BLK), bf),
        pltpu.VMEM((416, QROWS), jnp.float32),
        pltpu.VMEM((NX, NX, SLOT, W), bf),
        pltpu.VMEM((2, W, 8 * 128), bf),
        pltpu.VMEM((NX * NX, NX, SLOT, 128), bf),
        pltpu.VMEM((NX * NX, NX, SLOT, 128), bf),
        *[pltpu.VMEM((2, NX, n, SLOT, lanes), bf) for n, lanes in group_shapes],
        *[pltpu.VMEM((NX, n, SLOT, lanes), bf) for n, lanes in group_shapes],
        *[pltpu.VMEM((2, 3, n, SLOT // 2, lanes), bf) for n, lanes in group_shapes],
        dma((2, NPIECE + ND)), dma((2, NPIECE + ND)),
        dma((2, NPIECE + ND)), dma((2, NPIECE + ND)),
        dma((2, 2)), dma((2, 2)),
        dma((4,)), dma((4,)),
        dma((4, 2, 3)), dma((4, 2, 3)),
        dma((2, NX * NX - 1)), dma((2, NX * NX - 1)),
    ]
    return pl.pallas_call(
        kernel,
        out_shape=jax.ShapeDtypeStruct((800, W), jnp.float32),
        in_specs=[smem, smem, smem, smem, vmem, vmem, vmem],
        out_specs=vmem,
        scratch_shapes=scratch,
        compiler_params=pltpu.CompilerParams(
            collective_id=0, has_side_effects=True, vmem_limit_bytes=64 * 1024 * 1024
        ),
    )(block_sizes, int_pattern, occ_pattern, vir_pattern, ints, occ_density, vir_density)


def solution(mesh):
    return jax.shard_map(
        local,
        mesh=mesh,
        in_specs=(P("row", None, None, None, "col"), P(), P(), P(), P(), P(), P()),
        out_specs=P("row", "col"),
        check_vma=False,
    )
```

```python
import jax
import jax.numpy as jnp
from jax import lax
from jax.experimental import pallas as pl
from jax.experimental.pallas import tpu as pltpu
from jax.sharding import PartitionSpec as P

BLK = 32
ND = 3
PB = 100
NB = 8
NX = 4
W = 400
SUB = 50
SLOT = 64
PIECE = 512
NPIECE = 6
LANES = 256
PARTS = (12, 12, 12, 14)
BASE = (0, 96, 192, 288)
PART_ROWS = (96, 96, 96, 112)
TILE = 16
QOFF = (0, 400, 800)
QFAR = (1280, 1376, 1536, 1632)
QROWS = 1792
MESH = pl.DeviceIdType.MESH
NT = (((1,), (1,)), ((), ()))
NN = (((1,), (0,)), ((), ()))
NEAR = ((0, 0, 0, 400), (1, 400, 0, 400), (2, 800, 0, 400))
FAR_A, FAR_B = (3, 1280, 0, 192), (3, 1536, 192, 208)
ALL = (0, 1, 2, 3)
GROUPS = (
    ((0,), ALL, 0, 1280, NEAR),
    ((1, 2), ALL, 0, 1280, NEAR),
    ((0, 1, 2), ALL, 1280, 256, (FAR_A,)),
    ((0, 1, 2), ALL, 1536, 256, (FAR_B,)),
    ((3,), (0, 1), 0, 1792, (*NEAR, FAR_A, FAR_B)),
    ((3,), (2, 3), 0, 1792, (*NEAR, FAR_A, FAR_B)),
)
NG = len(GROUPS)


def iota(shape, dim):
    return lax.broadcasted_iota(jnp.int32, shape, dim)


def dot(a, b, dims=NN):
    return lax.dot_general(a, b, dims, preferred_element_type=jnp.float32)


def function_of(v):
    part = (v >= BASE[1]).astype(jnp.int32) + (v >= BASE[2]).astype(jnp.int32) + (v >= BASE[3]).astype(jnp.int32)
    rest = v - BASE[1] * part
    owner = jnp.where(part == 3, rest // PARTS[3], rest // PARTS[0])
    return owner, PARTS[0] * part + rest - owner * jnp.where(part == 3, PARTS[3], PARTS[0])


def wrap(v, n=NX):
    return lax.rem(v + n, n)


def kernel(sizes, ri, occ_pat, vir_pat, ints_hbm, occ, vir, out, *scratch):
    ints, right, left, mixed, halo, occ_mat, vir_mat, match, acc, fin, one_hot, place, choose, wide, msgs, got = scratch[:16]
    parts, cores, hops = scratch[16 : 16 + NG], scratch[16 + NG : 16 + 2 * NG], scratch[16 + 2 * NG : 16 + 3 * NG]
    (
        i_sem, r_send, r_recv, rf_send, rf_recv, l_send, l_recv, lf_send, lf_recv,
        h_send, h_recv, c_send, c_recv, x_send, x_recv, a_send, a_recv,
    ) = scratch[16 + 3 * NG :]
    row = lax.axis_index("row")
    col = lax.axis_index("col")
    x, k = row // 2, lax.rem(row, 2)
    y, z = col // NX, lax.rem(col, NX)
    bf = jnp.bfloat16

    def at(nx, nk, ny, nz):
        return (2 * nx + nk, NX * ny + nz)

    up_x, down_x, far_x = wrap(x + 1), wrap(x - 1), wrap(x + 2)
    y_dev = (at(x, k, wrap(y + 1), z), at(x, k, wrap(y - 1), z))
    z_dev = (at(x, k, y, wrap(z + 1)), at(x, k, y, wrap(z - 1)))
    x_dev = (at(up_x, k, y, z), at(down_x, k, y, z))
    other = at(x, 1 - k, y, z)
    far_halo = (wrap(row + 2 * k - 1, NB), col)

    barrier = pltpu.get_barrier_semaphore()
    for target in (other, far_halo, *x_dev):
        pl.semaphore_signal(barrier, inc=1, device_id=target, device_id_type=MESH)

    def greet(n, _):
        target = (row, NX * wrap(y + n // NX) + wrap(z + lax.rem(n, NX)))
        pl.semaphore_signal(barrier, inc=1, device_id=target, device_id_type=MESH)
        return 0

    lax.fori_loop(1, NX * NX, greet, 0)
    loads = [pltpu.make_async_copy(ints_hbm.at[e], ints.at[e], i_sem.at[e]) for e in range(ND)]
    for load in loads:
        load.start()

    def remote(src, dst, send, recv, target):
        return pltpu.make_async_remote_copy(
            src_ref=src, dst_ref=dst, send_sem=send, recv_sem=recv, device_id=target, device_id_type=MESH
        )

    inner = ((iota((LANES, BLK), 0) & 31) == iota((LANES, BLK), 1)).astype(bf)
    same = (iota((LANES, LANES), 0) >> 5) == (iota((LANES, LANES), 1) >> 5)

    def spread_occ(n, _):
        e, f = n // ND, lax.rem(n, ND)
        j = wrap(row + e - 1, NB)
        block = (occ[j, f].astype(jnp.float32) * occ_pat[f, j].astype(jnp.float32)).astype(bf)
        full = dot(dot(inner, block).astype(bf), inner, NT)
        occ_mat[n] = jnp.where(same, full, 0.0).astype(bf)
        return 0

    lax.fori_loop(0, ND * ND, spread_occ, 0)

    own_size = sizes[row]
    owner, function = function_of(iota((W, 1), 0))
    eye = iota((W, W), 1) == owner * SUB + function
    ri_block = iota((1, W), 1) // PB

    def turn(p, _):
        e = p // 2
        keep = jnp.zeros((1, W), jnp.float32)
        for q in range(W // PB):
            value = ri[e, row, (W // PB) * col + q].astype(jnp.float32)
            keep = jnp.where(ri_block == q, value, keep)
        diag = jnp.where(eye, keep, 0.0).astype(bf)
        lane = iota((1, PIECE), 1) + lax.rem(p, 2) * PIECE
        partner = sizes[wrap(row + e - 1, NB)]
        fill = jnp.where(((lane >> 5) < own_size) & ((lane & 31) < partner), 1.0, 0.0)
        rows = ints[e, pl.ds(pl.multiple_of(lax.rem(p, 2) * PIECE, PIECE), PIECE), :]
        right[p, 0:W, :] = (dot(diag, rows, NT) * fill).astype(bf)
        return 0

    for e in range(ND):
        loads[e].wait()
        lax.fori_loop(2 * e, 2 * e + 2, turn, 0)
    pl.semaphore_wait(barrier, NX * NX - 1 + 4)

    def gather_copies(view, far, sems, targets):
        send, recv, on_send, on_recv = sems
        own, onward = {}, {}
        for way in (0, 1):
            for p in range(NPIECE):
                own[way, p] = remote(
                    view(p, 1, 0, 0, W), view(p, 1, 1 + way, 0, W), send.at[way, p], recv.at[way, p], targets[way]
                )
            for late in (0, 1):
                part = 2 * late + way
                for band in range(ND):
                    onward[way, late, band] = remote(
                        view(2 * band, 2, 1 + way, BASE[part], PART_ROWS[part]),
                        far(2 * band, 2, part),
                        on_send.at[way, late, band],
                        on_recv.at[way, late, band],
                        targets[way],
                    )
        return own, onward

    def right_view(p, n, slot, first, rows):
        return right.at[pl.ds(p, n), pl.ds(QOFF[slot] + first, rows), :]

    def right_far(p, n, part):
        return right.at[pl.ds(p, n), pl.ds(QFAR[part], PART_ROWS[part]), :]

    def left_view(p, n, slot, first, rows):
        return left.at[pl.ds(p, n), slot, pl.ds(first, rows), :]

    def left_far(p, n, part):
        return left_view(p, n, 3, BASE[part], PART_ROWS[part])

    r_own, r_on = gather_copies(right_view, right_far, (r_send, r_recv, rf_send, rf_recv), y_dev)
    l_own, l_on = gather_copies(left_view, left_far, (l_send, l_recv, lf_send, lf_recv), z_dev)
    for p in range(NPIECE):
        for way in (0, 1):
            r_own[way, p].start()

    near, far = 2 - 2 * k, 2 * k
    halos = {}
    for n, (band, target) in enumerate(((1, other), (near, other), (1, far_halo), (far, far_halo))):
        halos[n] = remote(mixed.at[band], halo.at[n], h_send.at[n], h_recv.at[n], target)

    def mix(dm, pairs):
        def body(g, _):
            h, start = g // 2, pl.multiple_of(lax.rem(g, 2) * LANES, LANES)
            total = None
            for e, f in pairs:
                term = dot(right[2 * e + h, 0:W, pl.ds(start, LANES)], occ_mat[ND * e + f])
                total = term if total is None else total + term
            mixed[dm, :, pl.ds(pl.multiple_of(g * LANES, LANES), LANES)] = total.astype(bf)
            return 0

        lax.fori_loop(0, BLK * BLK // LANES, body, 0)

    mix(1, ((0, 2), (1, 1), (2, 0)))
    halos[0].start()
    halos[2].start()
    mix(near, ((near // 2, near + 1 - near // 2), (near // 2 + 1, near - near // 2)))
    halos[1].start()
    mix(far, ((far // 2, far + 1 - far // 2), (far // 2 + 1, far - far // 2)))
    halos[3].start()

    match[...] = jnp.where((iota(match.shape, 0) & 31) == (iota(match.shape, 1) & 31), 1.0, 0.0).astype(bf)
    outer = ((iota((BLK * BLK, BLK), 0) >> 5) == iota((BLK * BLK, BLK), 1)).astype(bf)

    def spread_vir(g):
        block = (vir[row, g].astype(jnp.float32) * vir_pat[g, row].astype(jnp.float32)).astype(bf)
        tall = dot(outer, block, NT).astype(bf)

        def body(part, _):
            columns = iota((LANES, BLK), 0) + part * LANES
            full = dot(tall, ((columns >> 5) == iota((LANES, BLK), 1)).astype(bf), NT)
            vir_mat[g, :, pl.ds(pl.multiple_of(part * LANES, LANES), LANES)] = full.astype(bf) * match[...]
            return 0

        lax.fori_loop(0, BLK * BLK // LANES, body, 0)

    def contract(order, terms):
        def body(h, _):
            columns = pl.ds(pl.multiple_of(h * PIECE, PIECE), PIECE)
            total = None
            for ref, index, g in terms:
                term = dot(ref[index], vir_mat[g, :, columns])
                total = term if total is None else total + term
            left[2 * order + h, 0] = total.astype(bf)
            return 0

        lax.fori_loop(0, 2, body, 0)
        for h in (0, 1):
            for way in (0, 1):
                l_own[way, 2 * order + h].start()

    bands = (near, far, 1)
    spread_vir(1)
    spread_vir(near)
    halos[0].wait_recv()
    contract(0, ((mixed, near, 1), (halo, 0, near)))
    spread_vir(far)
    halos[2].wait_recv()
    contract(1, ((mixed, far, 1), (halo, 2, far)))
    halos[1].wait_recv()
    halos[3].wait_recv()
    contract(2, ((mixed, 1, 1), (halo, 1, near), (halo, 3, far)))

    for yy in (0, 1):
        owner, function = function_of(iota((W, 1), 0))
        target = iota((W, 8 * 128), 1)
        one_hot[yy] = jnp.where(target == owner * 128 + yy * SUB + function, 1.0, 0.0).astype(bf)
    lane = iota((1, NX * 128), 1)
    inside = lane & 127
    late = (inside >= SUB).astype(jnp.int32)
    column = (4 * late + (lane >> 7)) * SUB + inside - SUB * late
    place[...] = jnp.where((inside < 2 * SUB) & (iota(place.shape, 0) == column), 1.0, 0.0).astype(bf)
    source = iota((NX * NX * SLOT, 1), 0)
    part = (source >> 4) & 3
    inside = source & 15
    target = (source >> 6) * SUB + PARTS[0] * part + inside
    real = inside < jnp.where(part == 3, PARTS[3], PARTS[0])
    choose[...] = jnp.where(real & (iota(choose.shape, 1) == target), 1.0, 0.0).astype(bf)
    for p in range(NPIECE):
        right[p, 1200:1280, :] = jnp.zeros((80, PIECE), bf)
        right[p, 1472:1536, :] = jnp.zeros((64, PIECE), bf)
        right[p, 1744:1792, :] = jnp.zeros((48, PIECE), bf)
    acc[W:, :] = jnp.zeros((acc.shape[0] - W, acc.shape[1]), jnp.float32)

    def product(slot, first, lanes, rows=(0, W), orders=(0, 1, 2), add=False):
        p_rows = pl.ds(rows[0], rows[1] - rows[0])

        def body(n, _):
            start = pl.multiple_of(n * LANES, LANES)
            q_rows = pl.ds(pl.multiple_of(first + n * LANES, LANES), LANES)
            total = acc[p_rows, pl.ds(start, LANES)] if add else None
            for order in orders:
                for h in (0, 1):
                    term = dot(left[2 * order + h, slot, p_rows, :], right[2 * bands[order] + h, q_rows, :], NT)
                    total = term if total is None else total + term
            acc[p_rows, pl.ds(start, LANES)] = total
            return 0

        lax.fori_loop(0, lanes // LANES, body, 0)

    def split(n, which):
        _, some, _, lanes, _ = GROUPS[n]
        for s in range(8):
            for i, part in enumerate(some):
                first = BASE[part] + s * PARTS[part]
                parts[n][s % 2, s // 2, which, TILE * i : TILE * i + TILE] = acc[first : first + TILE, 0:lanes].astype(bf)

    core_copy, hop_copy = {}, {}

    def core_start(n):
        core_copy[n] = remote(parts[n].at[1 - k], cores[n], c_send.at[n], c_recv.at[n], other)
        core_copy[n].start()

    def halves(n):
        half = TILE * len(GROUPS[n][1]) // 2
        return pl.ds(0, half), pl.ds(half, half)

    def hop(n, way, m, src):
        hop_copy[n, way, m] = remote(
            src, hops[n].at[way, m], x_send.at[n, way, m], x_recv.at[n, way, m], x_dev[way]
        )
        hop_copy[n, way, m].start()

    def stage1(n):
        ref, extra = parts[n], cores[n]
        low, high = halves(n)
        core_copy[n].wait_recv()
        mine = ref.at[k]

        def join(b):
            mine[b] = (mine[b].astype(jnp.float32) + extra[b].astype(jnp.float32)).astype(bf)

        join(far_x)
        hop(n, 0, 0, mine.at[far_x, :, low, :])
        hop(n, 1, 0, mine.at[far_x, :, high, :])
        join(up_x)
        hop(n, 0, 1, mine.at[up_x, :, high, :])
        join(down_x)
        hop(n, 1, 1, mine.at[down_x, :, low, :])
        join(x)

    def stage2(n):
        mine = parts[n].at[k]
        low, high = halves(n)
        for way, b, rows in ((0, up_x, low), (1, down_x, high)):
            hop_copy[n, way, 0].wait_recv()
            mine[b, :, rows, :] = (
                mine[b, :, rows, :].astype(jnp.float32) + hops[n][way, 0].astype(jnp.float32)
            ).astype(bf)
            hop(n, way, 2, mine.at[b, :, rows, :])

    def stage3(n):
        slots, some, first, _, q_pieces = GROUPS[n]
        mine = parts[n].at[k]
        low, high = halves(n)
        half = TILE * len(some) // 2
        for way in (0, 1):
            for m in (1, 2):
                hop_copy[n, way, m].wait_recv()
        for rows, one, two, start in ((low, 2, 1, 0), (high, 1, 2, half)):
            total = (
                mine[x, :, rows, :].astype(jnp.float32)
                + hops[n][0, one].astype(jnp.float32)
                + hops[n][1, two].astype(jnp.float32)
            )
            start += TILE * some[0]
            for i, slot in enumerate(slots):
                for q, lane, into, width in q_pieces:
                    there = wrap(y + (0, -1, 1, 2)[q])
                    block = total[i, :, lane - first : lane - first + width].astype(bf)
                    fin[slot, there, start : start + half, into : into + width] = block

    exchange = {}

    def exchange_start(n, slots, rows):
        rows = pl.ds(*rows)
        for slot in slots:
            for pair in (0, 1):
                low, high = fin[slot, 2 * pair, rows, :], fin[slot, 2 * pair + 1, rows, :]
                packed = (dot(low, one_hot[0]) + dot(high, one_hot[1])).astype(bf)
                for s in range(8):
                    target = NX * (s // 2) + 2 * (s % 2) + pair
                    msgs[target, slot, rows, :] = packed[:, 128 * s : 128 * s + 128]
        which = pl.ds(slots[0], len(slots))

        def copy(m):
            target = NX * wrap(y + m // NX) + wrap(z + lax.rem(m, NX))
            return remote(
                msgs.at[target, which, rows, :],
                got.at[col, which, rows, :],
                a_send.at[n, m - 1],
                a_recv.at[n, m - 1],
                (row, target),
            )

        exchange[n] = copy

        def begin(m, _):
            copy(m).start()
            return 0

        lax.fori_loop(1, NX * NX, begin, 0)
        for slot in slots:
            got[col, slot, rows, :] = msgs[col, slot, rows, :]

    def exchange_wait(n, what):
        def body(m, _):
            if what == "recv":
                exchange[n](m).wait_recv()
            else:
                exchange[n](m).wait_send()
            return 0

        lax.fori_loop(1, NX * NX, body, 0)

    def arrive(order, own, onward):
        for band in order:
            for way in (0, 1):
                own[way, 2 * band].wait_recv()
                own[way, 2 * band + 1].wait_recv()
                onward[way, 0, band].start()
        for band in order:
            for way in (0, 1):
                onward[way, 1, band].start()

    def far_arrive(onward, late, order):
        for band in order:
            for way in (0, 1):
                onward[way, late, band].wait_recv()

    every = (0, 1, 2)
    arrive(every, r_own, r_on)
    product(0, 0, 1280)
    split(0, 0)
    core_start(0)
    arrive(every, l_own, l_on)
    stage1(0)
    product(1, 0, 1280)
    split(1, 0)
    product(2, 0, 1280)
    split(1, 1)
    core_start(1)
    stage2(0)
    far_arrive(r_on, 0, every)
    for i, slot in enumerate(every):
        product(slot, 1280, 256)
        split(2, i)
    core_start(2)
    stage1(1)
    stage3(0)
    stage2(1)
    stage1(2)
    far_arrive(l_on, 0, every)
    stage3(1)
    stage2(2)
    far_arrive(r_on, 1, every)
    for i, slot in enumerate(every):
        product(slot, 1536, 256)
        split(3, i)
    core_start(3)
    early, late = (0, BASE[2]), (BASE[2], W)
    product(3, 0, 1792, early)
    split(4, 0)
    core_start(4)
    stage3(2)
    stage1(3)
    far_arrive(l_on, 1, (0,))
    product(3, 0, 1792, late, (0,))
    stage1(4)
    stage2(3)
    far_arrive(l_on, 1, (1,))
    product(3, 0, 1792, late, (1,), True)
    stage2(4)
    far_arrive(l_on, 1, (2,))
    product(3, 0, 1792, late, (2,), True)
    split(5, 0)
    core_start(5)
    stage3(3)
    exchange_start(0, every, (0, SLOT))
    stage1(5)
    stage3(4)
    exchange_start(1, (3,), (0, SLOT // 2))
    stage2(5)
    stage3(5)
    exchange_start(2, (3,), (SLOT // 2, SLOT // 2))

    for n in range(3):
        exchange_wait(n, "recv")
    slot_of = {0: 0, 3: 1, 1: 2, 2: 3}
    for yy in range(NX):
        rows = [
            jnp.concatenate([got[NX * yy + src, slot_of[(zz - src) % NX]] for src in range(NX)], axis=1)
            for zz in range(NX)
        ]
        wide[:, 256 * yy : 256 * yy + 256] = dot(place[...], jnp.concatenate(rows, axis=0), NT).astype(bf)
    out[...] = dot(wide[...], choose[...])

    for copies in (r_own, r_on, l_own, l_on, halos, core_copy, hop_copy):
        for copy in copies.values():
            copy.wait_send()
    for n in range(3):
        exchange_wait(n, "send")


def local(integrals, block_sizes, int_pattern, occ_density, occ_pattern, vir_density, vir_pattern):
    ints = integrals.reshape(ND, BLK * BLK, W)
    bf = jnp.bfloat16
    vmem = pl.BlockSpec(memory_space=pltpu.VMEM)
    smem = pl.BlockSpec(memory_space=pltpu.SMEM)
    dma = pltpu.SemaphoreType.DMA
    shapes = [(len(slots), TILE * len(some), lanes) for slots, some, _, lanes, _ in GROUPS]
    scratch = [
        pltpu.VMEM((ND, BLK * BLK, W), bf),
        pltpu.VMEM((NPIECE, QROWS, PIECE), bf),
        pltpu.VMEM((NPIECE, NX, W, PIECE), bf),
        pltpu.VMEM((ND, W, BLK * BLK), bf),
        pltpu.VMEM((4, W, BLK * BLK), bf),
        pltpu.VMEM((ND * ND, LANES, LANES), bf),
        pltpu.VMEM((ND, BLK * BLK, BLK * BLK), bf),
        pltpu.VMEM((BLK * BLK, LANES), bf),
        pltpu.VMEM((416, QROWS), jnp.float32),
        pltpu.VMEM((NX, NX, SLOT, W), bf),
        pltpu.VMEM((2, W, 8 * 128), bf),
        pltpu.VMEM((W, NX * 128), bf),
        pltpu.VMEM((NX * NX * SLOT, 800), bf),
        pltpu.VMEM((W, NX * NX * SLOT), bf),
        pltpu.VMEM((NX * NX, NX, SLOT, 128), bf),
        pltpu.VMEM((NX * NX, NX, SLOT, 128), bf),
        *[pltpu.VMEM((2, NX, n, rows, lanes), bf) for n, rows, lanes in shapes],
        *[pltpu.VMEM((NX, n, rows, lanes), bf) for n, rows, lanes in shapes],
        *[pltpu.VMEM((2, 3, n, rows // 2, lanes), bf) for n, rows, lanes in shapes],
        dma((ND,)),
        *[dma((2, NPIECE)), dma((2, NPIECE)), dma((2, 2, ND)), dma((2, 2, ND))] * 2,
        dma((4,)), dma((4,)),
        dma((NG,)), dma((NG,)),
        dma((NG, 2, 3)), dma((NG, 2, 3)),
        dma((3, NX * NX - 1)), dma((3, NX * NX - 1)),
    ]
    response = pl.pallas_call(
        kernel,
        out_shape=jax.ShapeDtypeStruct((W, 800), jnp.float32),
        in_specs=[smem, smem, smem, smem, pl.BlockSpec(memory_space=pl.ANY), vmem, vmem],
        out_specs=vmem,
        scratch_shapes=scratch,
        compiler_params=pltpu.CompilerParams(
            collective_id=0, has_side_effects=True, vmem_limit_bytes=64 * 1024 * 1024
        ),
    )(block_sizes, int_pattern.transpose(1, 0, 2), occ_pattern.T, vir_pattern.T, ints, occ_density, vir_density)
    return response.T


def solution(mesh):
    return jax.shard_map(
        local,
        mesh=mesh,
        in_specs=(P("row", None, None, None, "col"), P(), P(), P(), P(), P(), P()),
        out_specs=P("row", "col"),
        check_vma=False,
    )
```

```python
import jax
import jax.numpy as jnp
from jax import lax
from jax.experimental import pallas as pl
from jax.experimental.pallas import tpu as pltpu
from jax.sharding import PartitionSpec as P

BLK = 32
ND = 3
PB = 100
NB = 8
NX = 4
W = 400
SUB = 50
SLOT = 64
PIECE = 512
NPIECE = 6
LANES = 256
PARTS = (12, 12, 12, 14)
BASE = (0, 96, 192, 288)
PART_ROWS = (96, 96, 96, 112)
TILE = 16
QOFF = (0, 400, 800)
QFAR = (1280, 1376, 1536, 1632)
QROWS = 1792
MESH = pl.DeviceIdType.MESH
NT = (((1,), (1,)), ((), ()))
NN = (((1,), (0,)), ((), ()))
NEAR = ((0, 0, 0, 400), (1, 400, 0, 400), (2, 800, 0, 400))
FAR_A, FAR_B = (3, 1280, 0, 192), (3, 1536, 192, 208)
ALL = (0, 1, 2, 3)
GROUPS = (
    ((0,), ALL, 0, 1280, NEAR),
    ((1,), ALL, 0, 1280, NEAR),
    ((2,), ALL, 0, 1280, NEAR),
    ((0, 1, 2), ALL, 1280, 256, (FAR_A,)),
    ((0, 1, 2), ALL, 1536, 256, (FAR_B,)),
    ((3,), (0, 1), 0, 1792, (*NEAR, FAR_A, FAR_B)),
    ((3,), (2, 3), 0, 1792, (*NEAR, FAR_A, FAR_B)),
)
NG = len(GROUPS)


def iota(shape, dim):
    return lax.broadcasted_iota(jnp.int32, shape, dim)


def dot(a, b, dims=NN):
    return lax.dot_general(a, b, dims, preferred_element_type=jnp.float32)


def function_of(v):
    part = (v >= BASE[1]).astype(jnp.int32) + (v >= BASE[2]).astype(jnp.int32) + (v >= BASE[3]).astype(jnp.int32)
    rest = v - BASE[1] * part
    owner = jnp.where(part == 3, rest // PARTS[3], rest // PARTS[0])
    return owner, PARTS[0] * part + rest - owner * jnp.where(part == 3, PARTS[3], PARTS[0])


def wrap(v, n=NX):
    return lax.rem(v + n, n)


def kernel(sizes, ri, occ_pat, vir_pat, ints_hbm, occ, vir, out, *scratch):
    ints, right, left, mixed, halo, occ_mat, vir_mat, match, tall, acc, fin, one_hot, place, choose, wide, msgs, got = scratch[:17]
    parts, cores, hops = scratch[17 : 17 + NG], scratch[17 + NG : 17 + 2 * NG], scratch[17 + 2 * NG : 17 + 3 * NG]
    (
        i_sem, r_send, r_recv, rf_send, rf_recv, l_send, l_recv, lf_send, lf_recv,
        h_send, h_recv, c_send, c_recv, x_send, x_recv, a_send, a_recv, meet,
    ) = scratch[17 + 3 * NG :]
    row = lax.axis_index("row")
    col = lax.axis_index("col")
    x, k = row // 2, lax.rem(row, 2)
    y, z = col // NX, lax.rem(col, NX)
    bf = jnp.bfloat16

    def at(nx, nk, ny, nz):
        return (2 * nx + nk, NX * ny + nz)

    up_x, down_x, far_x = wrap(x + 1), wrap(x - 1), wrap(x + 2)
    y_dev = (at(x, k, wrap(y + 1), z), at(x, k, wrap(y - 1), z))
    z_dev = (at(x, k, y, wrap(z + 1)), at(x, k, y, wrap(z - 1)))
    x_dev = (at(up_x, k, y, z), at(down_x, k, y, z))
    other = at(x, 1 - k, y, z)
    far_halo = (wrap(row + 2 * k - 1, NB), col)

    barrier = pltpu.get_barrier_semaphore()
    for target in (other, far_halo, *y_dev, *z_dev, *x_dev):
        pl.semaphore_signal(barrier, inc=1, device_id=target, device_id_type=MESH)
    loads = [pltpu.make_async_copy(ints_hbm.at[e], ints.at[e], i_sem.at[e]) for e in range(ND)]
    for load in loads:
        load.start()

    def remote(src, dst, send, recv, target):
        return pltpu.make_async_remote_copy(
            src_ref=src, dst_ref=dst, send_sem=send, recv_sem=recv, device_id=target, device_id_type=MESH
        )

    inner = ((iota((LANES, BLK), 0) & 31) == iota((LANES, BLK), 1)).astype(bf)
    same = (iota((LANES, LANES), 0) >> 5) == (iota((LANES, LANES), 1) >> 5)

    def spread_occ(n, _):
        e, f = n // ND, lax.rem(n, ND)
        j = wrap(row + e - 1, NB)
        block = (occ[j, f].astype(jnp.float32) * occ_pat[f, j].astype(jnp.float32)).astype(bf)
        full = dot(dot(inner, block).astype(bf), inner, NT)
        occ_mat[n] = jnp.where(same, full, 0.0).astype(bf)
        return 0

    lax.fori_loop(0, ND, lambda n, c: spread_occ(2 * n + 2, c), 0)

    own_size = sizes[row]
    owner, function = function_of(iota((W, 1), 0))
    eye = iota((W, W), 1) == owner * SUB + function
    ri_block = iota((1, W), 1) // PB

    def turn(p, _):
        e = p // 2
        keep = jnp.zeros((1, W), jnp.float32)
        for q in range(W // PB):
            value = ri[e, row, (W // PB) * col + q].astype(jnp.float32)
            keep = jnp.where(ri_block == q, value, keep)
        diag = jnp.where(eye, keep, 0.0).astype(bf)
        lane = iota((1, PIECE), 1) + lax.rem(p, 2) * PIECE
        partner = sizes[wrap(row + e - 1, NB)]
        fill = jnp.where(((lane >> 5) < own_size) & ((lane & 31) < partner), 1.0, 0.0)
        rows = ints[e, pl.ds(pl.multiple_of(lax.rem(p, 2) * PIECE, PIECE), PIECE), :]
        right[p, 0:W, :] = (dot(diag, rows, NT) * fill).astype(bf)
        return 0

    for e in range(ND):
        loads[e].wait()
        lax.fori_loop(2 * e, 2 * e + 2, turn, 0)
    pl.semaphore_wait(barrier, 8)

    def meet_signal(n, targets):
        for target in targets:
            pl.semaphore_signal(meet.at[n], inc=1, device_id=target, device_id_type=MESH)

    def meet_wait(n):
        pl.semaphore_wait(meet.at[n], 2)

    meet_signal(0, y_dev)

    def gather_copies(view, far, sems, targets):
        send, recv, on_send, on_recv = sems
        own, onward = {}, {}
        for way in (0, 1):
            for p in range(NPIECE):
                own[way, p] = remote(
                    view(p, 1, 0, 0, W), view(p, 1, 1 + way, 0, W), send.at[way, p], recv.at[way, p], targets[way]
                )
            for late in (0, 1):
                part = 2 * late + way
                for band in range(ND):
                    onward[way, late, band] = remote(
                        view(2 * band, 2, 1 + way, BASE[part], PART_ROWS[part]),
                        far(2 * band, 2, part),
                        on_send.at[way, late, band],
                        on_recv.at[way, late, band],
                        targets[way],
                    )
        return own, onward

    def right_view(p, n, slot, first, rows):
        return right.at[pl.ds(p, n), pl.ds(QOFF[slot] + first, rows), :]

    def right_far(p, n, part):
        return right.at[pl.ds(p, n), pl.ds(QFAR[part], PART_ROWS[part]), :]

    def left_view(p, n, slot, first, rows):
        return left.at[pl.ds(p, n), slot, pl.ds(first, rows), :]

    def left_far(p, n, part):
        return left_view(p, n, 3, BASE[part], PART_ROWS[part])

    r_own, r_on = gather_copies(right_view, right_far, (r_send, r_recv, rf_send, rf_recv), y_dev)
    l_own, l_on = gather_copies(left_view, left_far, (l_send, l_recv, lf_send, lf_recv), z_dev)
    for p in range(NPIECE):
        for way in (0, 1):
            r_own[way, p].start()

    near, far = 2 - 2 * k, 2 * k
    halos = {}
    for n, (band, target) in enumerate(((1, other), (near, other), (1, far_halo), (far, far_halo))):
        halos[n] = remote(mixed.at[band], halo.at[n], h_send.at[n], h_recv.at[n], target)

    def mix(dm, pairs):
        def body(g, _):
            h, start = g // 2, pl.multiple_of(lax.rem(g, 2) * LANES, LANES)
            total = None
            for e, f in pairs:
                term = dot(right[2 * e + h, 0:W, pl.ds(start, LANES)], occ_mat[ND * e + f])
                total = term if total is None else total + term
            mixed[dm, :, pl.ds(pl.multiple_of(g * LANES, LANES), LANES)] = total.astype(bf)
            return 0

        lax.fori_loop(0, BLK * BLK // LANES, body, 0)

    mix(1, ((0, 2), (1, 1), (2, 0)))
    halos[0].start()
    halos[2].start()
    lax.fori_loop(0, 4, lambda n, c: spread_occ(2 * n + 1, c), 0)
    mix(near, ((near // 2, near + 1 - near // 2), (near // 2 + 1, near - near // 2)))
    halos[1].start()
    mix(far, ((far // 2, far + 1 - far // 2), (far // 2 + 1, far - far // 2)))
    halos[3].start()

    match[...] = jnp.where(iota(match.shape, 0) == (iota(match.shape, 1) & 31), 1.0, 0.0)
    repeat = ((iota((BLK, BLK * BLK), 1) >> 5) == iota((BLK, BLK * BLK), 0)).astype(bf)

    def spread_vir(g):
        block = (vir[row, g].astype(jnp.float32) * vir_pat[g, row].astype(jnp.float32)).astype(bf)
        tall[...] = dot(block, repeat, (((0,), (0,)), ((), ())))

        def body(a, _):
            rows = tall[pl.ds(a, 1), :] * match[...]
            vir_mat[g, pl.ds(pl.multiple_of(a * BLK, BLK), BLK), :] = rows.astype(bf)
            return 0

        lax.fori_loop(0, BLK, body, 0)

    def contract(order, terms):
        def body(h, _):
            columns = pl.ds(pl.multiple_of(h * PIECE, PIECE), PIECE)
            total = None
            for ref, index, g in terms:
                term = dot(ref[index], vir_mat[g, :, columns])
                total = term if total is None else total + term
            left[2 * order + h, 0] = total.astype(bf)
            return 0

        lax.fori_loop(0, 2, body, 0)
        for h in (0, 1):
            for way in (0, 1):
                l_own[way, 2 * order + h].start()

    meet_wait(0)
    meet_signal(1, z_dev)
    bands = (near, far, 1)
    spread_vir(1)
    spread_vir(near)
    halos[0].wait_recv()
    contract(0, ((mixed, near, 1), (halo, 0, near)))
    spread_vir(far)
    halos[2].wait_recv()
    contract(1, ((mixed, far, 1), (halo, 2, far)))
    halos[1].wait_recv()
    halos[3].wait_recv()
    contract(2, ((mixed, 1, 1), (halo, 1, near), (halo, 3, far)))

    for yy in (0, 1):
        owner, function = function_of(iota((W, 1), 0))
        target = iota((W, 8 * 128), 1)
        one_hot[yy] = jnp.where(target == owner * 128 + yy * SUB + function, 1.0, 0.0).astype(bf)
    lane = iota((1, NX * 128), 1)
    inside = lane & 127
    late = (inside >= SUB).astype(jnp.int32)
    column = (4 * late + (lane >> 7)) * SUB + inside - SUB * late
    place[...] = jnp.where((inside < 2 * SUB) & (iota(place.shape, 0) == column), 1.0, 0.0).astype(bf)
    source = iota((NX * NX * SLOT, 1), 0)
    part = (source >> 4) & 3
    inside = source & 15
    target = (source >> 6) * SUB + PARTS[0] * part + inside
    real = inside < jnp.where(part == 3, PARTS[3], PARTS[0])
    choose[...] = jnp.where(real & (iota(choose.shape, 1) == target), 1.0, 0.0).astype(bf)
    for p in range(NPIECE):
        right[p, 1200:1280, :] = jnp.zeros((80, PIECE), bf)
        right[p, 1472:1536, :] = jnp.zeros((64, PIECE), bf)
        right[p, 1744:1792, :] = jnp.zeros((48, PIECE), bf)
    acc[W:, :] = jnp.zeros((acc.shape[0] - W, acc.shape[1]), jnp.float32)

    def product(slot, first, lanes, rows=(0, W), orders=(0, 1, 2), add=False, into=0):
        p_rows = pl.ds(rows[0], rows[1] - rows[0])

        def body(n, _):
            start = pl.multiple_of(into + n * LANES, LANES)
            q_rows = pl.ds(pl.multiple_of(first + n * LANES, LANES), LANES)
            total = acc[p_rows, pl.ds(start, LANES)] if add else None
            for order in orders:
                for h in (0, 1):
                    term = dot(left[2 * order + h, slot, p_rows, :], right[2 * bands[order] + h, q_rows, :], NT)
                    total = term if total is None else total + term
            acc[p_rows, pl.ds(start, LANES)] = total
            return 0

        lax.fori_loop(0, lanes // LANES, body, 0)

    def split(n, which, lane=0):
        _, some, _, lanes, _ = GROUPS[n]
        for s in range(8):
            for i, part in enumerate(some):
                first = BASE[part] + s * PARTS[part]
                parts[n][s % 2, s // 2, which, TILE * i : TILE * i + TILE] = acc[first : first + TILE, lane : lane + lanes].astype(bf)

    core_copy, hop_copy = {}, {}

    def core_start(n):
        core_copy[n] = remote(parts[n].at[1 - k], cores[n], c_send.at[n], c_recv.at[n], other)
        core_copy[n].start()

    def halves(n):
        half = TILE * len(GROUPS[n][1]) // 2
        return pl.ds(0, half), pl.ds(half, half)

    def hop(n, way, m, src):
        hop_copy[n, way, m] = remote(
            src, hops[n].at[way, m], x_send.at[n, way, m], x_recv.at[n, way, m], x_dev[way]
        )
        hop_copy[n, way, m].start()

    def stage1(n):
        ref, extra = parts[n], cores[n]
        low, high = halves(n)
        core_copy[n].wait_recv()
        mine = ref.at[k]

        def join(b):
            mine[b] = (mine[b].astype(jnp.float32) + extra[b].astype(jnp.float32)).astype(bf)

        join(far_x)
        hop(n, 0, 0, mine.at[far_x, :, low, :])
        hop(n, 1, 0, mine.at[far_x, :, high, :])
        join(up_x)
        hop(n, 0, 1, mine.at[up_x, :, high, :])
        join(down_x)
        hop(n, 1, 1, mine.at[down_x, :, low, :])
        join(x)

    def stage2(n):
        mine = parts[n].at[k]
        low, high = halves(n)
        for way, b, rows in ((0, up_x, low), (1, down_x, high)):
            hop_copy[n, way, 0].wait_recv()
            mine[b, :, rows, :] = (
                mine[b, :, rows, :].astype(jnp.float32) + hops[n][way, 0].astype(jnp.float32)
            ).astype(bf)
            hop(n, way, 2, mine.at[b, :, rows, :])

    def stage3(n):
        slots, some, first, _, q_pieces = GROUPS[n]
        mine = parts[n].at[k]
        low, high = halves(n)
        half = TILE * len(some) // 2
        for way in (0, 1):
            for m in (1, 2):
                hop_copy[n, way, m].wait_recv()
        for rows, one, two, start in ((low, 2, 1, 0), (high, 1, 2, half)):
            total = (
                mine[x, :, rows, :].astype(jnp.float32)
                + hops[n][0, one].astype(jnp.float32)
                + hops[n][1, two].astype(jnp.float32)
            )
            start += TILE * some[0]
            for i, slot in enumerate(slots):
                for q, lane, into, width in q_pieces:
                    there = wrap(y + (0, -1, 1, 2)[q])
                    block = total[i, :, lane - first : lane - first + width].astype(bf)
                    fin[there, SLOT * slot + start : SLOT * slot + start + half, into : into + width] = block

    exchange = {}

    def exchange_start(n, slots):
        rows = pl.ds(SLOT * slots[0], SLOT * len(slots))
        for pair in (0, 1):
            packed = dot(fin[2 * pair, rows, :], one_hot[0]) + dot(fin[2 * pair + 1, rows, :], one_hot[1])
            packed = packed.astype(bf)
            for s in range(8):
                target = NX * (s // 2) + 2 * (s % 2) + pair
                msgs[target, rows, :] = packed[:, 128 * s : 128 * s + 128]

        def copy(m):
            target = NX * wrap(y + m // NX) + wrap(z + lax.rem(m, NX))
            return remote(
                msgs.at[target, rows, :], got.at[col, rows, :], a_send.at[n, m - 1], a_recv.at[n, m - 1], (row, target)
            )

        exchange[n] = copy

        def begin(m, _):
            copy(m).start()
            return 0

        lax.fori_loop(1, NX * NX, begin, 0)
        got[col, rows, :] = msgs[col, rows, :]

    def exchange_wait(n, what):
        def body(m, _):
            if what == "recv":
                exchange[n](m).wait_recv()
            else:
                exchange[n](m).wait_send()
            return 0

        lax.fori_loop(1, NX * NX, body, 0)

    def arrive(order, own, onward):
        for band in order:
            for way in (0, 1):
                own[way, 2 * band].wait_recv()
                own[way, 2 * band + 1].wait_recv()
                onward[way, 0, band].start()
        for band in order:
            for way in (0, 1):
                onward[way, 1, band].start()

    def far_arrive(onward, late, order):
        for band in order:
            for way in (0, 1):
                onward[way, late, band].wait_recv()

    every = (0, 1, 2)
    arrive(every, r_own, r_on)
    product(0, 0, 1280)
    split(0, 0)
    core_start(0)
    meet_wait(1)
    meet_signal(2, z_dev)
    stage1(0)
    arrive(every, l_own, l_on)
    product(1, 0, 1280)
    split(1, 0)
    core_start(1)
    stage2(0)
    product(2, 0, 1280)
    split(2, 0)
    core_start(2)
    stage1(1)
    meet_wait(2)
    far_arrive(r_on, 0, every)
    for i, slot in enumerate(every):
        product(slot, 1280, 256)
        split(3, i)
    core_start(3)
    stage1(2)
    stage2(1)
    stage3(0)
    early, late = (0, BASE[2]), (BASE[2], W)
    stage1(3)
    stage2(2)
    far_arrive(l_on, 0, every)
    product(3, 0, 1536, early)
    stage3(1)
    stage2(3)
    far_arrive(r_on, 1, every)
    product(3, 1536, 256, early, into=1536)
    split(5, 0)
    core_start(5)
    for i, slot in enumerate(every):
        product(slot, 1536, 256, into=1536)
        split(4, i, 1536)
    core_start(4)
    stage1(5)
    stage3(2)
    far_arrive(l_on, 1, (0,))
    product(3, 0, 1792, late, (0,))
    stage1(4)
    stage3(3)
    stage2(5)
    far_arrive(l_on, 1, (1,))
    product(3, 0, 1792, late, (1,), True)
    stage2(4)
    far_arrive(l_on, 1, (2,))
    product(3, 0, 1792, late, (2,), True)
    split(6, 0)
    core_start(6)
    stage3(5)
    stage3(4)
    stage1(6)
    exchange_start(0, every)
    stage2(6)
    stage3(6)
    exchange_start(1, (3,))

    for n in (0, 1):
        exchange_wait(n, "recv")
    slot_of = {0: 0, 3: 1, 1: 2, 2: 3}
    for yy in range(NX):
        rows = [
            jnp.concatenate([got[NX * yy + src, pl.ds(SLOT * slot_of[(zz - src) % NX], SLOT)] for src in range(NX)], axis=1)
            for zz in range(NX)
        ]
        wide[:, 256 * yy : 256 * yy + 256] = dot(place[...], jnp.concatenate(rows, axis=0), NT).astype(bf)
    out[...] = dot(wide[...], choose[...]).astype(bf)

    for copies in (r_own, r_on, l_own, l_on, halos, core_copy, hop_copy):
        for copy in copies.values():
            copy.wait_send()
    for n in (0, 1):
        exchange_wait(n, "send")


def local(integrals, block_sizes, int_pattern, occ_density, occ_pattern, vir_density, vir_pattern):
    ints = integrals.reshape(ND, BLK * BLK, W)
    bf = jnp.bfloat16
    vmem = pl.BlockSpec(memory_space=pltpu.VMEM)
    smem = pl.BlockSpec(memory_space=pltpu.SMEM)
    dma = pltpu.SemaphoreType.DMA
    shapes = [(len(slots), TILE * len(some), lanes) for slots, some, _, lanes, _ in GROUPS]
    scratch = [
        pltpu.VMEM((ND, BLK * BLK, W), bf),
        pltpu.VMEM((NPIECE, QROWS, PIECE), bf),
        pltpu.VMEM((NPIECE, NX, W, PIECE), bf),
        pltpu.VMEM((ND, W, BLK * BLK), bf),
        pltpu.VMEM((4, W, BLK * BLK), bf),
        pltpu.VMEM((ND * ND, LANES, LANES), bf),
        pltpu.VMEM((ND, BLK * BLK, BLK * BLK), bf),
        pltpu.VMEM((BLK, BLK * BLK), jnp.float32),
        pltpu.VMEM((BLK, BLK * BLK), jnp.float32),
        pltpu.VMEM((416, QROWS), jnp.float32),
        pltpu.VMEM((NX, NX * SLOT, W), bf),
        pltpu.VMEM((2, W, 8 * 128), bf),
        pltpu.VMEM((W, NX * 128), bf),
        pltpu.VMEM((NX * NX * SLOT, 800), bf),
        pltpu.VMEM((W, NX * NX * SLOT), bf),
        pltpu.VMEM((NX * NX, NX * SLOT, 128), bf),
        pltpu.VMEM((NX * NX, NX * SLOT, 128), bf),
        *[pltpu.VMEM((2, NX, n, rows, lanes), bf) for n, rows, lanes in shapes],
        *[pltpu.VMEM((NX, n, rows, lanes), bf) for n, rows, lanes in shapes],
        *[pltpu.VMEM((2, 3, n, rows // 2, lanes), bf) for n, rows, lanes in shapes],
        dma((ND,)),
        *[dma((2, NPIECE)), dma((2, NPIECE)), dma((2, 2, ND)), dma((2, 2, ND))] * 2,
        dma((4,)), dma((4,)),
        dma((NG,)), dma((NG,)),
        dma((NG, 2, 3)), dma((NG, 2, 3)),
        dma((2, NX * NX - 1)), dma((2, NX * NX - 1)),
        pltpu.SemaphoreType.REGULAR((3,)),
    ]
    response = pl.pallas_call(
        kernel,
        out_shape=jax.ShapeDtypeStruct((W, 800), bf),
        in_specs=[smem, smem, smem, smem, pl.BlockSpec(memory_space=pl.ANY), vmem, vmem],
        out_specs=vmem,
        scratch_shapes=scratch,
        compiler_params=pltpu.CompilerParams(
            collective_id=0, has_side_effects=True, vmem_limit_bytes=64 * 1024 * 1024
        ),
    )(block_sizes, int_pattern.transpose(1, 0, 2), occ_pattern.T, vir_pattern.T, ints, occ_density, vir_density)
    return response.astype(jnp.float32).T


def solution(mesh):
    return jax.shard_map(
        local,
        mesh=mesh,
        in_specs=(P("row", None, None, None, "col"), P(), P(), P(), P(), P(), P()),
        out_specs=P("row", "col"),
        check_vma=False,
    )
```

```python
import jax
import jax.numpy as jnp
from jax import lax
from jax.experimental import pallas as pl
from jax.experimental.pallas import tpu as pltpu
from jax.sharding import PartitionSpec as P

BLK = 32
ND = 3
PB = 100
NB = 8
NX = 4
W = 400
SUB = 50
SLOT = 64
PIECE = 512
NPIECE = 6
LANES = 256
PARTS = (12, 12, 12, 14)
BASE = (0, 96, 192, 288)
PART_ROWS = (96, 96, 96, 112)
TILE = 16
QOFF = (0, 400, 800)
QFAR = (1280, 1376, 1536, 1632)
QROWS = 1792
MESH = pl.DeviceIdType.MESH
NT = (((1,), (1,)), ((), ()))
NN = (((1,), (0,)), ((), ()))
NEAR = ((0, 0, 0, 400), (1, 400, 0, 400), (2, 800, 0, 400))
FAR_A, FAR_B = (3, 1280, 0, 192), (3, 1536, 192, 208)
ALL = (0, 1, 2, 3)
GROUPS = (
    ((0,), ALL, 0, 1280, NEAR),
    ((1,), ALL, 0, 1280, NEAR),
    ((2,), ALL, 0, 1280, NEAR),
    ((0, 1, 2), ALL, 1280, 256, (FAR_A,)),
    ((0, 1, 2), ALL, 1536, 256, (FAR_B,)),
    ((3,), (0, 1), 0, 1792, (*NEAR, FAR_A, FAR_B)),
    ((3,), (2, 3), 0, 1792, (*NEAR, FAR_A, FAR_B)),
)
NG = len(GROUPS)
PLACES = ((0, 0), (0, 1), (1, 1), (1, 2), (2, 2), (2, 3), (3, 3))


def iota(shape, dim):
    return lax.broadcasted_iota(jnp.int32, shape, dim)


def dot(a, b, dims=NN):
    return lax.dot_general(a, b, dims, preferred_element_type=jnp.float32)


def function_of(v):
    part = (v >= BASE[1]).astype(jnp.int32) + (v >= BASE[2]).astype(jnp.int32) + (v >= BASE[3]).astype(jnp.int32)
    rest = v - BASE[1] * part
    owner = jnp.where(part == 3, rest // PARTS[3], rest // PARTS[0])
    return owner, PARTS[0] * part + rest - owner * jnp.where(part == 3, PARTS[3], PARTS[0])


def wrap(v, n=NX):
    return lax.rem(v + n, n)


def kernel(sizes, ri, occ_pat, vir_pat, ints_hbm, occ, vir, out, *scratch):
    ints, right, left, mixed, halo, occ_mat, vir_mat, match, tall, acc, near_acc, fin, one_hot, place, choose, msgs, got = scratch[:17]
    parts, cores, hops = scratch[17 : 17 + NG], scratch[17 + NG : 17 + 2 * NG], scratch[17 + 2 * NG : 17 + 3 * NG]
    (
        i_sem, r_send, r_recv, rf_send, rf_recv, l_send, l_recv, lf_send, lf_recv,
        h_send, h_recv, c_send, c_recv, x_send, x_recv, a_send, a_recv, meet,
    ) = scratch[17 + 3 * NG :]
    row = lax.axis_index("row")
    col = lax.axis_index("col")
    x, k = row // 2, lax.rem(row, 2)
    y, z = col // NX, lax.rem(col, NX)
    bf = jnp.bfloat16

    def at(nx, nk, ny, nz):
        return (2 * nx + nk, NX * ny + nz)

    up_x, down_x, far_x = wrap(x + 1), wrap(x - 1), wrap(x + 2)
    y_dev = (at(x, k, wrap(y + 1), z), at(x, k, wrap(y - 1), z))
    z_dev = (at(x, k, y, wrap(z + 1)), at(x, k, y, wrap(z - 1)))
    x_dev = (at(up_x, k, y, z), at(down_x, k, y, z))
    other = at(x, 1 - k, y, z)
    far_halo = (wrap(row + 2 * k - 1, NB), col)

    near, far = 2 - 2 * k, 2 * k
    bands = (near, far, 1)
    barrier = pltpu.get_barrier_semaphore()
    for target in (other, far_halo, *y_dev, *z_dev, *x_dev):
        pl.semaphore_signal(barrier, inc=1, device_id=target, device_id_type=MESH)
    loads = []
    for p in range(NPIECE):
        rows = pl.ds(PIECE * (p % 2), PIECE)
        loads.append(pltpu.make_async_copy(ints_hbm.at[p // 2, rows, :], ints.at[p % 3], i_sem.at[p]))
    for load in loads[:3]:
        load.start()

    def remote(src, dst, send, recv, target):
        return pltpu.make_async_remote_copy(
            src_ref=src, dst_ref=dst, send_sem=send, recv_sem=recv, device_id=target, device_id_type=MESH
        )

    inner = ((iota((LANES, BLK), 0) & 31) == iota((LANES, BLK), 1)).astype(bf)
    same = (iota((LANES, LANES), 0) >> 5) == (iota((LANES, LANES), 1) >> 5)

    def spread_occ(n, _):
        e, f = n // ND, lax.rem(n, ND)
        j = wrap(row + e - 1, NB)
        block = (occ[j, f].astype(jnp.float32) * occ_pat[f, j].astype(jnp.float32)).astype(bf)
        full = dot(dot(inner, block).astype(bf), inner, NT)
        occ_mat[n - 1] = jnp.where(same, full, 0.0).astype(bf)
        return 0

    lax.fori_loop(0, ND, lambda n, c: spread_occ(2 * n + 2, c), 0)

    own_size = sizes[row]
    owner, function = function_of(iota((W, 1), 0))
    eye = iota((W, W), 1) == owner * SUB + function
    ri_block = iota((1, W), 1) // PB

    def turn(p):
        e = p // 2
        keep = jnp.zeros((1, W), jnp.float32)
        for q in range(W // PB):
            value = ri[e, row, (W // PB) * col + q].astype(jnp.float32)
            keep = jnp.where(ri_block == q, value, keep)
        diag = jnp.where(eye, keep, 0.0).astype(bf)
        lane = iota((1, PIECE), 1) + p % 2 * PIECE
        partner = sizes[wrap(row + e - 1, NB)]
        fill = jnp.where(((lane >> 5) < own_size) & ((lane & 31) < partner), 1.0, 0.0)
        right[p, 0:W, :] = (dot(diag, ints[p % 3], NT) * fill).astype(bf)

    for p in range(NPIECE):
        loads[p].wait()
        turn(p)
        if p + 3 < NPIECE:
            loads[p + 3].start()
    pl.semaphore_wait(barrier, 8)

    def meet_signal(n, targets):
        for target in targets:
            pl.semaphore_signal(meet.at[n], inc=1, device_id=target, device_id_type=MESH)

    def meet_wait(n):
        pl.semaphore_wait(meet.at[n], 2)

    meet_signal(0, y_dev)

    def gather_copies(view, far_view, sems, targets):
        send, recv, on_send, on_recv = sems
        own, onward = {}, {}
        for way in (0, 1):
            for q in range(NPIECE):
                own[way, q] = remote(
                    view(q, 1, 0, 0, W), view(q, 1, 1 + way, 0, W), send.at[way, q], recv.at[way, q], targets[way]
                )
            for late in (0, 1):
                part = 2 * late + way
                for order in range(ND):
                    onward[way, late, order] = remote(
                        view(2 * order, 2, 1 + way, BASE[part], PART_ROWS[part]),
                        far_view(2 * order, 2, part),
                        on_send.at[way, late, order],
                        on_recv.at[way, late, order],
                        targets[way],
                    )
        return own, onward

    def right_view(q, n, slot, first, rows):
        return right.at[pl.ds(2 * bands[q // 2] + q % 2, n), pl.ds(QOFF[slot] + first, rows), :]

    def right_far(q, n, part):
        return right.at[pl.ds(2 * bands[q // 2], n), pl.ds(QFAR[part], PART_ROWS[part]), :]

    def left_view(p, n, slot, first, rows):
        return left.at[pl.ds(p, n), slot, pl.ds(first, rows), :]

    def left_far(p, n, part):
        return left_view(p, n, 3, BASE[part], PART_ROWS[part])

    r_own, r_on = gather_copies(right_view, right_far, (r_send, r_recv, rf_send, rf_recv), y_dev)
    l_own, l_on = gather_copies(left_view, left_far, (l_send, l_recv, lf_send, lf_recv), z_dev)
    for p in range(NPIECE):
        for way in (0, 1):
            r_own[way, p].start()

    halos = {}
    for n, (band, target) in enumerate(((1, other), (near, other), (1, far_halo), (far, far_halo))):
        halos[n] = remote(mixed.at[band], halo.at[n], h_send.at[n], h_recv.at[n], target)

    def mix(dm, pairs):
        def body(g, _):
            h, start = g // 2, pl.multiple_of(lax.rem(g, 2) * LANES, LANES)
            total = None
            for e, f in pairs:
                term = dot(right[2 * e + h, 0:W, pl.ds(start, LANES)], occ_mat[ND * e + f - 1])
                total = term if total is None else total + term
            mixed[dm, :, pl.ds(pl.multiple_of(g * LANES, LANES), LANES)] = total.astype(bf)
            return 0

        lax.fori_loop(0, BLK * BLK // LANES, body, 0)

    mix(1, ((0, 2), (1, 1), (2, 0)))
    halos[0].start()
    halos[2].start()
    lax.fori_loop(0, 4, lambda n, c: spread_occ(2 * n + 1, c), 0)
    mix(near, ((near // 2, near + 1 - near // 2), (near // 2 + 1, near - near // 2)))
    halos[1].start()
    mix(far, ((far // 2, far + 1 - far // 2), (far // 2 + 1, far - far // 2)))
    halos[3].start()

    match[...] = jnp.where(iota(match.shape, 0) == (iota(match.shape, 1) & 31), 1.0, 0.0)
    repeat = ((iota((BLK, BLK * BLK), 1) >> 5) == iota((BLK, BLK * BLK), 0)).astype(bf)

    def spread_vir(g):
        block = (vir[row, g].astype(jnp.float32) * vir_pat[g, row].astype(jnp.float32)).astype(bf)
        tall[...] = dot(block, repeat, (((0,), (0,)), ((), ())))

        def body(a, _):
            rows = tall[pl.ds(a, 1), :] * match[...]
            vir_mat[g, pl.ds(pl.multiple_of(a * BLK, BLK), BLK), :] = rows.astype(bf)
            return 0

        lax.fori_loop(0, BLK, body, 0)

    def contract(order, terms):
        def body(h, _):
            columns = pl.ds(pl.multiple_of(h * PIECE, PIECE), PIECE)
            total = None
            for ref, index, g in terms:
                term = dot(ref[index], vir_mat[g, :, columns])
                total = term if total is None else total + term
            left[2 * order + h, 0] = total.astype(bf)
            return 0

        lax.fori_loop(0, 2, body, 0)
        for h in (0, 1):
            for way in (0, 1):
                l_own[way, 2 * order + h].start()

    meet_wait(0)
    meet_signal(1, z_dev)
    spread_vir(1)
    spread_vir(near)
    halos[0].wait_recv()
    contract(0, ((mixed, near, 1), (halo, 0, near)))
    spread_vir(far)
    halos[2].wait_recv()
    contract(1, ((mixed, far, 1), (halo, 2, far)))
    halos[1].wait_recv()
    halos[3].wait_recv()
    contract(2, ((mixed, 1, 1), (halo, 1, near), (halo, 3, far)))

    owner, function = function_of(iota((W, 1), 0))
    one_hot[...] = jnp.where(iota((W, 8 * 128), 1) == owner * 128 + function, 1.0, 0.0).astype(bf)
    lane = iota((1, NX * 128), 1)
    inside = lane & 127
    late = (inside >= SUB).astype(jnp.int32)
    column = (4 * late + (lane >> 7)) * SUB + inside - SUB * late
    place[...] = jnp.where((inside < 2 * SUB) & (iota(place.shape, 0) == column), 1.0, 0.0).astype(bf)
    source = iota((NX * SLOT, 1), 0)
    part = (source >> 4) & 3
    inside = source & 15
    target = (source >> 6) * SUB + PARTS[0] * part + inside
    real = inside < jnp.where(part == 3, PARTS[3], PARTS[0])
    for i, (n, yy) in enumerate(PLACES):
        lane = iota(choose.shape[1:], 1) + (LANES * n - NX * SUB * yy)
        choose[i] = jnp.where(real & (lane == target), 1.0, 0.0).astype(bf)
    for p in range(NPIECE):
        right[p, 1200:1280, :] = jnp.zeros((80, PIECE), bf)
        right[p, 1472:1536, :] = jnp.zeros((64, PIECE), bf)
        right[p, 1744:1792, :] = jnp.zeros((48, PIECE), bf)
    acc[W:, :] = jnp.zeros((acc.shape[0] - W, acc.shape[1]), jnp.float32)
    near_acc[2 * W :, :] = jnp.zeros((near_acc.shape[0] - 2 * W, near_acc.shape[1]), jnp.float32)

    def product(slot, count, first, lanes, total, rows=(0, W), orders=(0, 1, 2), add=False, into=0):
        p_rows = pl.ds(rows[0], rows[1] - rows[0])
        out_rows = p_rows if count == 1 else pl.ds(0, W * count)

        def left_rows(piece):
            if count == 1:
                return left[piece, slot, p_rows, :]
            return left[piece, slot : slot + count].reshape(count * W, PIECE)

        def body(n, _):
            lane = pl.ds(pl.multiple_of(into + n * LANES, LANES), LANES)
            q_rows = pl.ds(pl.multiple_of(first + n * LANES, LANES), LANES)
            value = total[out_rows, lane] if add else None
            for order in orders:
                for h in (0, 1):
                    term = dot(left_rows(2 * order + h), right[2 * bands[order] + h, q_rows, :], NT)
                    value = term if value is None else value + term
            total[out_rows, lane] = value
            return 0

        lax.fori_loop(0, lanes // LANES, body, 0)

    def split(n, which, total, row=0, lane=0):
        _, some, _, lanes, _ = GROUPS[n]
        for s in range(8):
            for i, part in enumerate(some):
                first = row + BASE[part] + s * PARTS[part]
                parts[n][s % 2, s // 2, which, TILE * i : TILE * i + TILE] = total[first : first + TILE, lane : lane + lanes].astype(bf)

    core_copy, hop_copy = {}, {}

    def core_start(n):
        core_copy[n] = remote(parts[n].at[1 - k], cores[n], c_send.at[n], c_recv.at[n], other)
        core_copy[n].start()

    def halves(n):
        half = TILE * len(GROUPS[n][1]) // 2
        return pl.ds(0, half), pl.ds(half, half)

    def hop(n, way, m, src):
        hop_copy[n, way, m] = remote(
            src, hops[n].at[way, m], x_send.at[n, way, m], x_recv.at[n, way, m], x_dev[way]
        )
        hop_copy[n, way, m].start()

    def stage1(n):
        ref, extra = parts[n], cores[n]
        low, high = halves(n)
        core_copy[n].wait_recv()
        mine = ref.at[k]

        def join(b):
            mine[b] = (mine[b].astype(jnp.float32) + extra[b].astype(jnp.float32)).astype(bf)

        join(far_x)
        hop(n, 0, 0, mine.at[far_x, :, low, :])
        hop(n, 1, 0, mine.at[far_x, :, high, :])
        join(up_x)
        hop(n, 0, 1, mine.at[up_x, :, high, :])
        join(down_x)
        hop(n, 1, 1, mine.at[down_x, :, low, :])
        join(x)

    def stage2(n):
        mine = parts[n].at[k]
        low, high = halves(n)
        for way, b, rows in ((0, up_x, low), (1, down_x, high)):
            hop_copy[n, way, 0].wait_recv()
            mine[b, :, rows, :] = (
                mine[b, :, rows, :].astype(jnp.float32) + hops[n][way, 0].astype(jnp.float32)
            ).astype(bf)
            hop(n, way, 2, mine.at[b, :, rows, :])

    def stage3(n):
        slots, some, first, _, q_pieces = GROUPS[n]
        mine = parts[n].at[k]
        low, high = halves(n)
        half = TILE * len(some) // 2
        for way in (0, 1):
            for m in (1, 2):
                hop_copy[n, way, m].wait_recv()
        for rows, one, two, start in ((low, 2, 1, 0), (high, 1, 2, half)):
            total = (
                mine[x, :, rows, :].astype(jnp.float32)
                + hops[n][0, one].astype(jnp.float32)
                + hops[n][1, two].astype(jnp.float32)
            )
            start += TILE * some[0]
            for i, slot in enumerate(slots):
                for q, lane, into, width in q_pieces:
                    there = wrap(y + (0, -1, 1, 2)[q])
                    block = total[i, :, lane - first : lane - first + width].astype(bf)
                    rows_in = pl.ds(SLOT * slot + start, half)
                    fin[lax.rem(there, 2), there // 2, rows_in, into : into + width] = block

    exchange = {}

    own_pair = y // 2

    def exchange_start(n, first, count, pairs, some=None):
        rows = pl.ds(first, count)
        packed = None
        for yy in (0, 1):
            chunks = [fin[yy, pair, rows, :] for pair in pairs]
            term = dot(chunks[0] if len(chunks) == 1 else jnp.concatenate(chunks, axis=0), one_hot[...])
            packed = term if packed is None else packed + pltpu.roll(term, SUB, 1)
        packed = packed.astype(bf)
        for i, pair in enumerate(pairs):
            for s in range(8):
                target = NX * (s // 2) + 2 * (s % 2) + pair
                msgs[target, rows, :] = packed[count * i : count * (i + 1), 128 * s : 128 * s + 128]

        def copy(m):
            target = NX * wrap(y + m // NX) + wrap(z + lax.rem(m, NX))
            return remote(
                msgs.at[target, rows, :], got.at[col, rows, :], a_send.at[n, m - 1], a_recv.at[n, m - 1], (row, target)
            )

        exchange[n] = copy

        def begin(m, _):
            if some is None:
                copy(m).start()
            else:

                @pl.when(lax.rem(z + m, 2) == some)
                def _():
                    copy(m).start()

            return 0

        lax.fori_loop(1, NX * NX, begin, 0)

    def exchange_wait(n, what):
        def body(m, _):
            if what == "recv":
                exchange[n](m).wait_recv()
            else:
                exchange[n](m).wait_send()
            return 0

        lax.fori_loop(1, NX * NX, body, 0)

    def arrive(order, own, onward):
        for way in (0, 1):
            own[way, 2 * order].wait_recv()
            own[way, 2 * order + 1].wait_recv()
            onward[way, 0, order].start()

    def pass_late(onward):
        for order in range(ND):
            for way in (0, 1):
                onward[way, 1, order].start()

    def far_arrive(onward, late, orders=(0, 1, 2)):
        for order in orders:
            for way in (0, 1):
                onward[way, late, order].wait_recv()

    for order in range(ND):
        arrive(order, r_own, r_on)
        if order == ND - 1:
            pass_late(r_on)
        product(0, 1, 0, 1280, acc, orders=(order,), add=order > 0)
    split(0, 0, acc)
    core_start(0)
    meet_wait(1)
    meet_signal(2, z_dev)
    for order in range(ND):
        arrive(order, l_own, l_on)
        if order == ND - 1:
            pass_late(l_on)
        product(1, 2, 0, 1280, near_acc, orders=(order,), add=order > 0)
        if order == 0:
            stage1(0)
        if order == 1:
            stage2(0)
    split(1, 0, near_acc)
    core_start(1)
    split(2, 0, near_acc, W)
    core_start(2)
    meet_wait(2)
    stage1(1)
    far_arrive(r_on, 0)
    product(1, 2, 1280, 256, near_acc)
    product(0, 1, 1280, 256, near_acc, into=256)
    split(3, 0, near_acc, 0, 256)
    split(3, 1, near_acc)
    split(3, 2, near_acc, W)
    core_start(3)
    stage1(2)
    stage2(1)
    stage3(0)
    stage1(3)
    stage2(2)
    early, late = (0, BASE[2]), (BASE[2], W)
    far_arrive(l_on, 0)
    product(3, 1, 0, 1536, acc, early)
    stage3(1)
    stage2(3)
    far_arrive(r_on, 1)
    product(3, 1, 1536, 256, acc, early, into=1536)
    split(5, 0, acc)
    core_start(5)
    product(1, 2, 1536, 256, near_acc)
    product(0, 1, 1536, 256, near_acc, into=256)
    split(4, 0, near_acc, 0, 256)
    split(4, 1, near_acc)
    split(4, 2, near_acc, W)
    core_start(4)
    stage1(5)
    stage3(2)
    far_arrive(l_on, 1, (0,))
    product(3, 1, 0, 1792, acc, late, (0,))
    stage1(4)
    stage3(3)
    stage2(5)
    far_arrive(l_on, 1, (1,))
    product(3, 1, 0, 1792, acc, late, (1,), True)
    stage2(4)
    exchange_start(0, 0, 3 * SLOT, (own_pair,), own_pair)
    far_arrive(l_on, 1, (2,))
    product(3, 1, 0, 1792, acc, late, (2,), True)
    split(6, 0, acc)
    core_start(6)
    stage3(5)
    stage3(4)
    stage1(6)
    exchange_start(0, 0, 3 * SLOT, (1 - own_pair,), 1 - own_pair)
    stage2(6)
    exchange_start(1, 3 * SLOT, SLOT // 2, (0, 1))
    stage3(6)
    exchange_start(2, 3 * SLOT + SLOT // 2, SLOT // 2, (0, 1))
    got[col] = msgs[col]

    for n in (0, 1, 2):
        exchange_wait(n, "recv")
    slot_of = {0: 0, 3: 1, 1: 2, 2: 3}
    for copy in halos.values():
        copy.wait_send()
    wide = mixed.at[0]
    for yy in range(NX):
        rows = [
            jnp.concatenate([got[NX * yy + src, pl.ds(SLOT * slot_of[(zz - src) % NX], SLOT)] for src in range(NX)], axis=1)
            for zz in range(NX)
        ]
        wide[:, 256 * yy : 256 * yy + 256] = dot(place[...], jnp.concatenate(rows, axis=0), NT).astype(bf)
    for n in range(4):
        width = min(LANES, 800 - LANES * n)
        total = None
        for i, (tile, yy) in enumerate(PLACES):
            if tile == n:
                term = dot(wide[:, 256 * yy : 256 * yy + 256], choose[i, :, 0:width])
                total = term if total is None else total + term
        out[:, LANES * n : LANES * n + width] = total.astype(bf)

    for copies in (r_own, r_on, l_own, l_on, core_copy, hop_copy):
        for copy in copies.values():
            copy.wait_send()
    for n in (0, 1, 2):
        exchange_wait(n, "send")


def local(integrals, block_sizes, int_pattern, occ_density, occ_pattern, vir_density, vir_pattern):
    ints = integrals.reshape(ND, BLK * BLK, W)
    bf = jnp.bfloat16
    vmem = pl.BlockSpec(memory_space=pltpu.VMEM)
    smem = pl.BlockSpec(memory_space=pltpu.SMEM)
    dma = pltpu.SemaphoreType.DMA
    shapes = [(len(slots), TILE * len(some), lanes) for slots, some, _, lanes, _ in GROUPS]
    scratch = [
        pltpu.VMEM((3, PIECE, W), bf),
        pltpu.VMEM((NPIECE, QROWS, PIECE), bf),
        pltpu.VMEM((NPIECE, NX, W, PIECE), bf),
        pltpu.VMEM((ND, W, BLK * BLK), bf),
        pltpu.VMEM((4, W, BLK * BLK), bf),
        pltpu.VMEM((ND * ND - 2, LANES, LANES), bf),
        pltpu.VMEM((ND, BLK * BLK, BLK * BLK), bf),
        pltpu.VMEM((BLK, BLK * BLK), jnp.float32),
        pltpu.VMEM((BLK, BLK * BLK), jnp.float32),
        pltpu.VMEM((416, QROWS), jnp.float32),
        pltpu.VMEM((2 * W + 16, 1280), jnp.float32),
        pltpu.VMEM((2, 2, NX * SLOT, W), bf),
        pltpu.VMEM((W, 8 * 128), bf),
        pltpu.VMEM((W, NX * 128), bf),
        pltpu.VMEM((len(PLACES), LANES, LANES), bf),
        pltpu.VMEM((NX * NX, NX * SLOT, 128), bf),
        pltpu.VMEM((NX * NX, NX * SLOT, 128), bf),
        *[pltpu.VMEM((2, NX, n, rows, lanes), bf) for n, rows, lanes in shapes],
        *[pltpu.VMEM((NX, n, rows, lanes), bf) for n, rows, lanes in shapes],
        *[pltpu.VMEM((2, 3, n, rows // 2, lanes), bf) for n, rows, lanes in shapes],
        dma((NPIECE,)),
        *[dma((2, NPIECE)), dma((2, NPIECE)), dma((2, 2, ND)), dma((2, 2, ND))] * 2,
        dma((4,)), dma((4,)),
        dma((NG,)), dma((NG,)),
        dma((NG, 2, 3)), dma((NG, 2, 3)),
        dma((3, NX * NX - 1)), dma((3, NX * NX - 1)),
        pltpu.SemaphoreType.REGULAR((3,)),
    ]
    response = pl.pallas_call(
        kernel,
        out_shape=jax.ShapeDtypeStruct((W, 800), bf),
        in_specs=[smem, smem, smem, smem, pl.BlockSpec(memory_space=pl.ANY), vmem, vmem],
        out_specs=vmem,
        scratch_shapes=scratch,
        compiler_params=pltpu.CompilerParams(
            collective_id=0, has_side_effects=True, vmem_limit_bytes=64 * 1024 * 1024
        ),
    )(block_sizes, int_pattern.transpose(1, 0, 2), occ_pattern.T, vir_pattern.T, ints, occ_density, vir_density)
    return response.astype(jnp.float32).T


def solution(mesh):
    return jax.shard_map(
        local,
        mesh=mesh,
        in_specs=(P("row", None, None, None, "col"), P(), P(), P(), P(), P(), P()),
        out_specs=P("row", "col"),
        check_vma=False,
    )
```

```python
import jax
import jax.numpy as jnp
from jax import lax
from jax.experimental import pallas as pl
from jax.experimental.pallas import tpu as pltpu
from jax.sharding import PartitionSpec as P

BLK = 32
ND = 3
PB = 100
NB = 8
NX = 4
W = 400
SUB = 50
SLOT = 64
PIECE = 512
NPIECE = 6
LANES = 256
PARTS = (12, 12, 12, 14)
BASE = (0, 96, 192, 288)
PART_ROWS = (96, 96, 96, 112)
TILE = 16
QOFF = (0, 400, 800)
QFAR = (1280, 1376, 1536, 1632)
QROWS = 1792
MESH = pl.DeviceIdType.MESH
NT = (((1,), (1,)), ((), ()))
NN = (((1,), (0,)), ((), ()))
NEAR = ((0, 0, 0, 400), (1, 400, 0, 400), (2, 800, 0, 400))
FAR_A, FAR_B = (3, 1280, 0, 192), (3, 1536, 192, 208)
ALL = (0, 1, 2, 3)
GROUPS = (
    ((0,), ALL, 0, 1280, NEAR),
    ((1,), ALL, 0, 1280, NEAR),
    ((2,), ALL, 0, 1280, NEAR),
    ((0, 1, 2), ALL, 1280, 256, (FAR_A,)),
    ((0, 1, 2), ALL, 1536, 256, (FAR_B,)),
    ((3,), (0, 1), 0, 1792, (*NEAR, FAR_A, FAR_B)),
    ((3,), (2, 3), 0, 1792, (*NEAR, FAR_A, FAR_B)),
)
NG = len(GROUPS)
FAR_FIRST = (10, 6, 14, 9, 11, 2, 8, 5, 7, 13, 15, 1, 3, 4, 12)
PLACES = ((0, 0), (0, 1), (1, 1), (1, 2), (2, 2), (2, 3), (3, 3))


def iota(shape, dim):
    return lax.broadcasted_iota(jnp.int32, shape, dim)


def dot(a, b, dims=NN):
    return lax.dot_general(a, b, dims, preferred_element_type=jnp.float32)


def function_of(v):
    part = (v >= BASE[1]).astype(jnp.int32) + (v >= BASE[2]).astype(jnp.int32) + (v >= BASE[3]).astype(jnp.int32)
    rest = v - BASE[1] * part
    owner = jnp.where(part == 3, rest // PARTS[3], rest // PARTS[0])
    return owner, PARTS[0] * part + rest - owner * jnp.where(part == 3, PARTS[3], PARTS[0])


def wrap(v, n=NX):
    return lax.rem(v + n, n)


def kernel(sizes, ri, occ_pat, vir_pat, ints_hbm, occ, vir, out, *scratch):
    ints, right, left, mixed, halo, occ_mat, vir_mat, match, tall, acc, near_acc, fin, one_hot, place, choose, msgs, got = scratch[:17]
    parts, cores, hops = scratch[17 : 17 + NG], scratch[17 + NG : 17 + 2 * NG], scratch[17 + 2 * NG : 17 + 3 * NG]
    (
        i_sem, r_send, r_recv, rf_send, rf_recv, l_send, l_recv, lf_send, lf_recv,
        h_send, h_recv, c_send, c_recv, x_send, x_recv, a_send, a_recv, meet,
    ) = scratch[17 + 3 * NG :]
    row = lax.axis_index("row")
    col = lax.axis_index("col")
    x, k = row // 2, lax.rem(row, 2)
    y, z = col // NX, lax.rem(col, NX)
    bf = jnp.bfloat16

    def at(nx, nk, ny, nz):
        return (2 * nx + nk, NX * ny + nz)

    up_x, down_x, far_x = wrap(x + 1), wrap(x - 1), wrap(x + 2)
    y_dev = (at(x, k, wrap(y + 1), z), at(x, k, wrap(y - 1), z))
    z_dev = (at(x, k, y, wrap(z + 1)), at(x, k, y, wrap(z - 1)))
    x_dev = (at(up_x, k, y, z), at(down_x, k, y, z))
    other = at(x, 1 - k, y, z)
    far_halo = (wrap(row + 2 * k - 1, NB), col)

    near, far = 2 - 2 * k, 2 * k
    bands = (near, far, 1)
    barrier = pltpu.get_barrier_semaphore()
    for target in (other, far_halo, *y_dev, *z_dev, *x_dev):
        pl.semaphore_signal(barrier, inc=1, device_id=target, device_id_type=MESH)
    loads = []
    for p in range(NPIECE):
        rows = pl.ds(PIECE * (p % 2), PIECE)
        loads.append(pltpu.make_async_copy(ints_hbm.at[p // 2, rows, :], ints.at[p % 3], i_sem.at[p]))
    for load in loads[:3]:
        load.start()

    def remote(src, dst, send, recv, target):
        return pltpu.make_async_remote_copy(
            src_ref=src, dst_ref=dst, send_sem=send, recv_sem=recv, device_id=target, device_id_type=MESH
        )

    inner = ((iota((LANES, BLK), 0) & 31) == iota((LANES, BLK), 1)).astype(bf)
    same = (iota((LANES, LANES), 0) >> 5) == (iota((LANES, LANES), 1) >> 5)

    def spread_occ(n, _):
        e, f = n // ND, lax.rem(n, ND)
        j = wrap(row + e - 1, NB)
        block = (occ[j, f].astype(jnp.float32) * occ_pat[f, j].astype(jnp.float32)).astype(bf)
        full = dot(dot(inner, block).astype(bf), inner, NT)
        occ_mat[n - 1] = jnp.where(same, full, 0.0).astype(bf)
        return 0

    lax.fori_loop(0, ND, lambda n, c: spread_occ(2 * n + 2, c), 0)

    own_size = sizes[row]
    owner, function = function_of(iota((W, 1), 0))
    eye = iota((W, W), 1) == owner * SUB + function
    ri_block = iota((1, W), 1) // PB

    def keep_of(e):
        keep = jnp.zeros((1, W), jnp.float32)
        for q in range(W // PB):
            value = ri[e, row, (W // PB) * col + q].astype(jnp.float32)
            keep = jnp.where(ri_block == q, value, keep)
        return jnp.where(eye, keep, 0.0).astype(bf)

    def turn(p, diag):
        lane = iota((1, PIECE), 1) + p % 2 * PIECE
        partner = sizes[wrap(row + p // 2 - 1, NB)]
        fill = jnp.where(((lane >> 5) < own_size) & ((lane & 31) < partner), 1.0, 0.0)
        right[p, 0:W, :] = (dot(diag, ints[p % 3], NT) * fill).astype(bf)

    diag = None
    for p in range(NPIECE):
        if p % 2 == 0:
            diag = keep_of(p // 2)
        loads[p].wait()
        turn(p, diag)
        if p + 3 < NPIECE:
            loads[p + 3].start()
    pl.semaphore_wait(barrier, 8)

    def meet_signal(n, targets):
        for target in targets:
            pl.semaphore_signal(meet.at[n], inc=1, device_id=target, device_id_type=MESH)

    def meet_wait(n):
        pl.semaphore_wait(meet.at[n], 2)

    meet_signal(0, y_dev)

    def gather_copies(view, far_view, sems, targets):
        send, recv, on_send, on_recv = sems
        own, onward = {}, {}
        for way in (0, 1):
            for q in range(NPIECE):
                own[way, q] = remote(
                    view(q, 1, 0, 0, W), view(q, 1, 1 + way, 0, W), send.at[way, q], recv.at[way, q], targets[way]
                )
            for late in (0, 1):
                part = 2 * late + way
                for order in range(ND):
                    onward[way, late, order] = remote(
                        view(2 * order, 2, 1 + way, BASE[part], PART_ROWS[part]),
                        far_view(2 * order, 2, part),
                        on_send.at[way, late, order],
                        on_recv.at[way, late, order],
                        targets[way],
                    )
        return own, onward

    def right_view(q, n, slot, first, rows):
        return right.at[pl.ds(2 * bands[q // 2] + q % 2, n), pl.ds(QOFF[slot] + first, rows), :]

    def right_far(q, n, part):
        return right.at[pl.ds(2 * bands[q // 2], n), pl.ds(QFAR[part], PART_ROWS[part]), :]

    def left_view(p, n, slot, first, rows):
        return left.at[pl.ds(p, n), slot, pl.ds(first, rows), :]

    def left_far(p, n, part):
        return left_view(p, n, 3, BASE[part], PART_ROWS[part])

    r_own, r_on = gather_copies(right_view, right_far, (r_send, r_recv, rf_send, rf_recv), y_dev)
    l_own, l_on = gather_copies(left_view, left_far, (l_send, l_recv, lf_send, lf_recv), z_dev)
    for p in range(NPIECE):
        for way in (0, 1):
            r_own[way, p].start()

    halos = {}
    for n, (band, target) in enumerate(((1, other), (near, other), (1, far_halo), (far, far_halo))):
        halos[n] = remote(mixed.at[band], halo.at[n], h_send.at[n], h_recv.at[n], target)

    def mix(dm, pairs):
        def body(g, _):
            h, start = g // 2, pl.multiple_of(lax.rem(g, 2) * LANES, LANES)
            total = None
            for e, f in pairs:
                term = dot(right[2 * e + h, 0:W, pl.ds(start, LANES)], occ_mat[ND * e + f - 1])
                total = term if total is None else total + term
            mixed[dm, :, pl.ds(pl.multiple_of(g * LANES, LANES), LANES)] = total.astype(bf)
            return 0

        lax.fori_loop(0, BLK * BLK // LANES, body, 0)

    mix(1, ((0, 2), (1, 1), (2, 0)))
    halos[0].start()
    halos[2].start()
    lax.fori_loop(0, 4, lambda n, c: spread_occ(2 * n + 1, c), 0)
    mix(near, ((near // 2, near + 1 - near // 2), (near // 2 + 1, near - near // 2)))
    halos[1].start()

    match[...] = jnp.where(iota(match.shape, 0) == (iota(match.shape, 1) & 31), 1.0, 0.0)
    repeat = ((iota((BLK, BLK * BLK), 1) >> 5) == iota((BLK, BLK * BLK), 0)).astype(bf)

    def spread_vir(g):
        block = (vir[row, g].astype(jnp.float32) * vir_pat[g, row].astype(jnp.float32)).astype(bf)
        tall[...] = dot(block, repeat, (((0,), (0,)), ((), ())))

        def body(a, _):
            rows = tall[pl.ds(a, 1), :] * match[...]
            vir_mat[g, pl.ds(pl.multiple_of(a * BLK, BLK), BLK), :] = rows.astype(bf)
            return 0

        lax.fori_loop(0, BLK, body, 0)

    def contract(order, terms):
        for h in (0, 1):
            total = None
            for ref, index, g in terms:
                term = dot(ref[index], vir_mat[g, :, PIECE * h : PIECE * (h + 1)])
                total = term if total is None else total + term
            left[2 * order + h, 0] = total.astype(bf)
            for way in (0, 1):
                l_own[way, 2 * order + h].start()

    meet_wait(0)
    meet_signal(1, z_dev)
    spread_vir(1)
    spread_vir(near)
    halos[0].wait_recv()
    contract(0, ((mixed, near, 1), (halo, 0, near)))
    mix(far, ((far // 2, far + 1 - far // 2), (far // 2 + 1, far - far // 2)))
    halos[3].start()
    spread_vir(far)
    halos[2].wait_recv()
    contract(1, ((mixed, far, 1), (halo, 2, far)))
    halos[1].wait_recv()
    halos[3].wait_recv()
    contract(2, ((mixed, 1, 1), (halo, 1, near), (halo, 3, far)))

    owner, function = function_of(iota((W, 1), 0))
    one_hot[...] = jnp.where(iota((W, 8 * 128), 1) == owner * 128 + function, 1.0, 0.0).astype(bf)
    lane = iota((1, NX * 128), 1)
    inside = lane & 127
    late = (inside >= SUB).astype(jnp.int32)
    column = (4 * late + (lane >> 7)) * SUB + inside - SUB * late
    place[...] = jnp.where((inside < 2 * SUB) & (iota(place.shape, 0) == column), 1.0, 0.0).astype(bf)
    source = iota((NX * SLOT, 1), 0)
    part = (source >> 4) & 3
    inside = source & 15
    target = (source >> 6) * SUB + PARTS[0] * part + inside
    real = inside < jnp.where(part == 3, PARTS[3], PARTS[0])
    for i, (n, yy) in enumerate(PLACES):
        lane = iota(choose.shape[1:], 1) + (LANES * n - NX * SUB * yy)
        choose[i] = jnp.where(real & (lane == target), 1.0, 0.0).astype(bf)
    for p in range(NPIECE):
        right[p, 1200:1280, :] = jnp.zeros((80, PIECE), bf)
        right[p, 1472:1536, :] = jnp.zeros((64, PIECE), bf)
        right[p, 1744:1792, :] = jnp.zeros((48, PIECE), bf)
    acc[W:, :] = jnp.zeros((acc.shape[0] - W, acc.shape[1]), jnp.float32)
    near_acc[2 * W :, :] = jnp.zeros((near_acc.shape[0] - 2 * W, near_acc.shape[1]), jnp.float32)

    def product(slot, count, first, lanes, total, rows=(0, W), orders=(0, 1, 2), add=False, into=0):
        p_rows = pl.ds(rows[0], rows[1] - rows[0])
        out_rows = p_rows if count == 1 else pl.ds(0, W * count)

        def left_rows(piece):
            if count == 1:
                return left[piece, slot, p_rows, :]
            return left[piece, slot : slot + count].reshape(count * W, PIECE)

        def body(n, _):
            lane = pl.ds(pl.multiple_of(into + n * LANES, LANES), LANES)
            q_rows = pl.ds(pl.multiple_of(first + n * LANES, LANES), LANES)
            value = total[out_rows, lane] if add else None
            for order in orders:
                for h in (0, 1):
                    term = dot(left_rows(2 * order + h), right[2 * bands[order] + h, q_rows, :], NT)
                    value = term if value is None else value + term
            total[out_rows, lane] = value
            return 0

        lax.fori_loop(0, lanes // LANES, body, 0)

    def split(n, which, total, row=0, lane=0):
        _, some, _, lanes, _ = GROUPS[n]
        for s in range(8):
            for i, part in enumerate(some):
                first = row + BASE[part] + s * PARTS[part]
                parts[n][s % 2, s // 2, which, TILE * i : TILE * i + TILE] = total[first : first + TILE, lane : lane + lanes].astype(bf)

    core_copy, hop_copy = {}, {}

    def core_start(n):
        core_copy[n] = remote(parts[n].at[1 - k], cores[n], c_send.at[n], c_recv.at[n], other)
        core_copy[n].start()

    def halves(n):
        half = TILE * len(GROUPS[n][1]) // 2
        return pl.ds(0, half), pl.ds(half, half)

    def hop(n, way, m, src):
        hop_copy[n, way, m] = remote(
            src, hops[n].at[way, m], x_send.at[n, way, m], x_recv.at[n, way, m], x_dev[way]
        )
        hop_copy[n, way, m].start()

    def stage1(n):
        ref, extra = parts[n], cores[n]
        low, high = halves(n)
        core_copy[n].wait_recv()
        mine = ref.at[k]

        def join(b):
            mine[b] = (mine[b].astype(jnp.float32) + extra[b].astype(jnp.float32)).astype(bf)

        join(far_x)
        hop(n, 0, 0, mine.at[far_x, :, low, :])
        hop(n, 1, 0, mine.at[far_x, :, high, :])
        join(up_x)
        hop(n, 0, 1, mine.at[up_x, :, high, :])
        join(down_x)
        hop(n, 1, 1, mine.at[down_x, :, low, :])
        join(x)

    def stage2(n):
        mine = parts[n].at[k]
        low, high = halves(n)
        for way, b, rows in ((0, up_x, low), (1, down_x, high)):
            hop_copy[n, way, 0].wait_recv()
            mine[b, :, rows, :] = (
                mine[b, :, rows, :].astype(jnp.float32) + hops[n][way, 0].astype(jnp.float32)
            ).astype(bf)
            hop(n, way, 2, mine.at[b, :, rows, :])

    def stage3(n):
        slots, some, first, _, q_pieces = GROUPS[n]
        mine = parts[n].at[k]
        low, high = halves(n)
        half = TILE * len(some) // 2
        for way in (0, 1):
            for m in (1, 2):
                hop_copy[n, way, m].wait_recv()
        for rows, one, two, start in ((low, 2, 1, 0), (high, 1, 2, half)):
            total = (
                mine[x, :, rows, :].astype(jnp.float32)
                + hops[n][0, one].astype(jnp.float32)
                + hops[n][1, two].astype(jnp.float32)
            )
            start += TILE * some[0]
            for i, slot in enumerate(slots):
                for q, lane, into, width in q_pieces:
                    there = wrap(y + (0, -1, 1, 2)[q])
                    block = total[i, :, lane - first : lane - first + width].astype(bf)
                    rows_in = pl.ds(SLOT * slot + start, half)
                    fin[lax.rem(there, 2), there // 2, rows_in, into : into + width] = block

    exchange = {}

    own_pair = y // 2

    def exchange_start(n, first, count, pairs, some=None):
        rows = pl.ds(first, count)
        packed = None
        for yy in (0, 1):
            chunks = [fin[yy, pair, rows, :] for pair in pairs]
            term = dot(chunks[0] if len(chunks) == 1 else jnp.concatenate(chunks, axis=0), one_hot[...])
            packed = term if packed is None else packed + pltpu.roll(term, SUB, 1)
        packed = packed.astype(bf)
        for i, pair in enumerate(pairs):
            for s in range(8):
                target = NX * (s // 2) + 2 * (s % 2) + pair
                msgs[target, rows, :] = packed[count * i : count * (i + 1), 128 * s : 128 * s + 128]

        def copy(m):
            target = NX * wrap(y + m // NX) + wrap(z + lax.rem(m, NX))
            return remote(
                msgs.at[target, rows, :], got.at[col, rows, :], a_send.at[n, m - 1], a_recv.at[n, m - 1], (row, target)
            )

        exchange[n] = copy

        for m in FAR_FIRST:
            if some is None:
                copy(m).start()
            else:
                pl.when(lax.rem(z + m, 2) == some)(copy(m).start)

    def exchange_wait(n, what):
        for m in FAR_FIRST:
            if what == "recv":
                exchange[n](m).wait_recv()
            else:
                exchange[n](m).wait_send()

    def arrive(order, own, onward):
        for way in (0, 1):
            own[way, 2 * order].wait_recv()
            own[way, 2 * order + 1].wait_recv()
            onward[way, 0, order].start()

    def pass_late(onward):
        for order in range(ND):
            for way in (0, 1):
                onward[way, 1, order].start()

    def far_arrive(onward, late, orders=(0, 1, 2)):
        for order in orders:
            for way in (0, 1):
                onward[way, late, order].wait_recv()

    for order in range(ND):
        arrive(order, r_own, r_on)
        if order == ND - 1:
            pass_late(r_on)
        product(0, 1, 0, 1280, acc, orders=(order,), add=order > 0)
    split(0, 0, acc)
    core_start(0)
    meet_wait(1)
    meet_signal(2, z_dev)
    for order in range(ND):
        arrive(order, l_own, l_on)
        if order == ND - 1:
            pass_late(l_on)
        product(1, 2, 0, 1280, near_acc, orders=(order,), add=order > 0)
        if order == 0:
            stage1(0)
        if order == 1:
            stage2(0)
    split(1, 0, near_acc)
    core_start(1)
    split(2, 0, near_acc, W)
    core_start(2)
    meet_wait(2)
    stage1(1)
    far_arrive(r_on, 0)
    product(1, 2, 1280, 256, near_acc)
    product(0, 1, 1280, 256, near_acc, into=256)
    split(3, 0, near_acc, 0, 256)
    split(3, 1, near_acc)
    split(3, 2, near_acc, W)
    core_start(3)
    stage1(2)
    stage2(1)
    stage3(0)
    stage1(3)
    stage2(2)
    early, late = (0, BASE[2]), (BASE[2], W)
    far_arrive(l_on, 0)
    product(3, 1, 0, 1536, acc, early)
    stage3(1)
    stage2(3)
    far_arrive(r_on, 1)
    product(3, 1, 1536, 256, acc, early, into=1536)
    split(5, 0, acc)
    core_start(5)
    product(1, 2, 1536, 256, near_acc)
    product(0, 1, 1536, 256, near_acc, into=256)
    split(4, 0, near_acc, 0, 256)
    split(4, 1, near_acc)
    split(4, 2, near_acc, W)
    core_start(4)
    stage1(5)
    stage3(2)
    far_arrive(l_on, 1, (0,))
    product(3, 1, 0, 1792, acc, late, (0,))
    stage1(4)
    stage3(3)
    stage2(5)
    far_arrive(l_on, 1, (1,))
    product(3, 1, 0, 1792, acc, late, (1,), True)
    stage2(4)
    exchange_start(0, 0, 3 * SLOT, (own_pair,), own_pair)
    far_arrive(l_on, 1, (2,))
    product(3, 1, 0, 1792, acc, late, (2,), True)
    split(6, 0, acc)
    core_start(6)
    stage1(6)
    stage3(5)
    stage3(4)
    exchange_start(0, 0, 3 * SLOT, (1 - own_pair,), 1 - own_pair)
    stage2(6)
    stage3(6)
    exchange_start(1, 3 * SLOT, SLOT, (0, 1))
    got[col] = msgs[col]

    for n in (0, 1):
        exchange_wait(n, "recv")
    slot_of = {0: 0, 3: 1, 1: 2, 2: 3}
    for copy in halos.values():
        copy.wait_send()
    wide = mixed.at[0]
    for yy in range(NX):
        rows = [
            jnp.concatenate([got[NX * yy + src, pl.ds(SLOT * slot_of[(zz - src) % NX], SLOT)] for src in range(NX)], axis=1)
            for zz in range(NX)
        ]
        wide[:, 256 * yy : 256 * yy + 256] = dot(place[...], jnp.concatenate(rows, axis=0), NT).astype(bf)
    for n in range(4):
        width = min(LANES, 800 - LANES * n)
        total = None
        for i, (tile, yy) in enumerate(PLACES):
            if tile == n:
                term = dot(wide[:, 256 * yy : 256 * yy + 256], choose[i, :, 0:width])
                total = term if total is None else total + term
        out[:, LANES * n : LANES * n + width] = total.astype(bf)

    for copies in (r_own, r_on, l_own, l_on, core_copy, hop_copy):
        for copy in copies.values():
            copy.wait_send()
    for n in (0, 1):
        exchange_wait(n, "send")


def local(integrals, block_sizes, int_pattern, occ_density, occ_pattern, vir_density, vir_pattern):
    ints = integrals.reshape(ND, BLK * BLK, W)
    bf = jnp.bfloat16
    vmem = pl.BlockSpec(memory_space=pltpu.VMEM)
    smem = pl.BlockSpec(memory_space=pltpu.SMEM)
    dma = pltpu.SemaphoreType.DMA
    shapes = [(len(slots), TILE * len(some), lanes) for slots, some, _, lanes, _ in GROUPS]
    scratch = [
        pltpu.VMEM((3, PIECE, W), bf),
        pltpu.VMEM((NPIECE, QROWS, PIECE), bf),
        pltpu.VMEM((NPIECE, NX, W, PIECE), bf),
        pltpu.VMEM((ND, W, BLK * BLK), bf),
        pltpu.VMEM((4, W, BLK * BLK), bf),
        pltpu.VMEM((ND * ND - 2, LANES, LANES), bf),
        pltpu.VMEM((ND, BLK * BLK, BLK * BLK), bf),
        pltpu.VMEM((BLK, BLK * BLK), jnp.float32),
        pltpu.VMEM((BLK, BLK * BLK), jnp.float32),
        pltpu.VMEM((416, QROWS), jnp.float32),
        pltpu.VMEM((2 * W + 16, 1280), jnp.float32),
        pltpu.VMEM((2, 2, NX * SLOT, W), bf),
        pltpu.VMEM((W, 8 * 128), bf),
        pltpu.VMEM((W, NX * 128), bf),
        pltpu.VMEM((len(PLACES), LANES, LANES), bf),
        pltpu.VMEM((NX * NX, NX * SLOT, 128), bf),
        pltpu.VMEM((NX * NX, NX * SLOT, 128), bf),
        *[pltpu.VMEM((2, NX, n, rows, lanes), bf) for n, rows, lanes in shapes],
        *[pltpu.VMEM((NX, n, rows, lanes), bf) for n, rows, lanes in shapes],
        *[pltpu.VMEM((2, 3, n, rows // 2, lanes), bf) for n, rows, lanes in shapes],
        dma((NPIECE,)),
        *[dma((2, NPIECE)), dma((2, NPIECE)), dma((2, 2, ND)), dma((2, 2, ND))] * 2,
        dma((4,)), dma((4,)),
        dma((NG,)), dma((NG,)),
        dma((NG, 2, 3)), dma((NG, 2, 3)),
        dma((2, NX * NX - 1)), dma((2, NX * NX - 1)),
        pltpu.SemaphoreType.REGULAR((3,)),
    ]
    response = pl.pallas_call(
        kernel,
        out_shape=jax.ShapeDtypeStruct((W, 800), bf),
        in_specs=[smem, smem, smem, smem, pl.BlockSpec(memory_space=pl.ANY), vmem, vmem],
        out_specs=vmem,
        scratch_shapes=scratch,
        compiler_params=pltpu.CompilerParams(
            collective_id=0, has_side_effects=True, vmem_limit_bytes=64 * 1024 * 1024
        ),
    )(block_sizes, int_pattern.transpose(1, 0, 2), occ_pattern.T, vir_pattern.T, ints, occ_density, vir_density)
    return response.astype(jnp.float32).T


def solution(mesh):
    return jax.shard_map(
        local,
        mesh=mesh,
        in_specs=(P("row", None, None, None, "col"), P(), P(), P(), P(), P(), P()),
        out_specs=P("row", "col"),
        check_vma=False,
    )
```

```python
import jax
import jax.numpy as jnp
from jax import lax
from jax.experimental import pallas as pl
from jax.experimental.pallas import tpu as pltpu
from jax.sharding import PartitionSpec as P

BLK = 32
ND = 3
PB = 100
NB = 8
NX = 4
W = 400
SUB = 50
SLOT = 64
PIECE = 512
NPIECE = 6
LANES = 256
PARTS = (12, 12, 12, 14)
BASE = (0, 96, 192, 288)
PART_ROWS = (96, 96, 96, 112)
TILE = 16
QOFF = (0, 400, 800)
QFAR = (1280, 1376, 1536, 1632)
QROWS = 1792
MESH = pl.DeviceIdType.MESH
NT = (((1,), (1,)), ((), ()))
NN = (((1,), (0,)), ((), ()))
NEAR = ((0, 0, 0, 400), (1, 400, 0, 400), (2, 800, 0, 400))
FAR_A, FAR_B = (3, 1280, 0, 192), (3, 1536, 192, 208)
ALL = (0, 1, 2, 3)
GROUPS = (
    ((0,), ALL, 0, 1280, NEAR),
    ((1,), ALL, 0, 1280, NEAR),
    ((2,), ALL, 0, 1280, NEAR),
    ((0, 1, 2), ALL, 1280, 256, (FAR_A,)),
    ((0, 1, 2), ALL, 1536, 256, (FAR_B,)),
    ((3,), (0, 1), 0, 1792, (*NEAR, FAR_A, FAR_B)),
    ((3,), (2, 3), 0, 1792, (*NEAR, FAR_A, FAR_B)),
)
NG = len(GROUPS)
FAR_FIRST = (10, 6, 14, 9, 11, 2, 8, 5, 7, 13, 15, 1, 3, 4, 12)
PLACES = ((0, 0), (0, 1), (1, 1), (1, 2), (2, 2), (2, 3), (3, 3))


def iota(shape, dim):
    return lax.broadcasted_iota(jnp.int32, shape, dim)


def dot(a, b, dims=NN):
    return lax.dot_general(a, b, dims, preferred_element_type=jnp.float32)


def function_of(v):
    part = (v >= BASE[1]).astype(jnp.int32) + (v >= BASE[2]).astype(jnp.int32) + (v >= BASE[3]).astype(jnp.int32)
    rest = v - BASE[1] * part
    owner = jnp.where(part == 3, rest // PARTS[3], rest // PARTS[0])
    return owner, PARTS[0] * part + rest - owner * jnp.where(part == 3, PARTS[3], PARTS[0])


def wrap(v, n=NX):
    return lax.rem(v + n, n)


def kernel(sizes, ri, occ_pat, vir_pat, ints_hbm, occ, vir, out, *scratch):
    ints, right, left, mixed, halo, occ_mat, vir_mat, match, tall, acc, near_acc, fin, one_hot, place, choose, msgs, got = scratch[:17]
    parts, cores, hops = scratch[17 : 17 + NG], scratch[17 + NG : 17 + 2 * NG], scratch[17 + 2 * NG : 17 + 3 * NG]
    (
        i_sem, r_send, r_recv, rf_send, rf_recv, l_send, l_recv, lf_send, lf_recv,
        h_send, h_recv, c_send, c_recv, x_send, x_recv, a_send, a_recv, meet,
    ) = scratch[17 + 3 * NG :]
    row = lax.axis_index("row")
    col = lax.axis_index("col")
    x, k = row // 2, lax.rem(row, 2)
    y, z = col // NX, lax.rem(col, NX)
    bf = jnp.bfloat16

    def at(nx, nk, ny, nz):
        return (2 * nx + nk, NX * ny + nz)

    up_x, down_x, far_x = wrap(x + 1), wrap(x - 1), wrap(x + 2)
    y_dev = (at(x, k, wrap(y + 1), z), at(x, k, wrap(y - 1), z))
    z_dev = (at(x, k, y, wrap(z + 1)), at(x, k, y, wrap(z - 1)))
    x_dev = (at(up_x, k, y, z), at(down_x, k, y, z))
    other = at(x, 1 - k, y, z)
    far_halo = (wrap(row + 2 * k - 1, NB), col)

    near, far = 2 - 2 * k, 2 * k
    bands = (near, far, 1)
    barrier = pltpu.get_barrier_semaphore()
    for target in (other, far_halo, *y_dev, *z_dev, *x_dev):
        pl.semaphore_signal(barrier, inc=1, device_id=target, device_id_type=MESH)
    loads = []
    for p in range(NPIECE):
        rows = pl.ds(PIECE * (p % 2), PIECE)
        loads.append(pltpu.make_async_copy(ints_hbm.at[p // 2, rows, :], ints.at[p % 3], i_sem.at[p]))
    for load in loads[:3]:
        load.start()

    def remote(src, dst, send, recv, target):
        return pltpu.make_async_remote_copy(
            src_ref=src, dst_ref=dst, send_sem=send, recv_sem=recv, device_id=target, device_id_type=MESH
        )

    inner = ((iota((LANES, BLK), 0) & 31) == iota((LANES, BLK), 1)).astype(bf)
    same = (iota((LANES, LANES), 0) >> 5) == (iota((LANES, LANES), 1) >> 5)

    def spread_occ(n, _):
        e, f = n // ND, lax.rem(n, ND)
        j = wrap(row + e - 1, NB)
        block = (occ[j, f].astype(jnp.float32) * occ_pat[f, j].astype(jnp.float32)).astype(bf)
        full = dot(dot(inner, block).astype(bf), inner, NT)
        occ_mat[n - 1] = jnp.where(same, full, 0.0).astype(bf)
        return 0

    lax.fori_loop(0, ND, lambda n, c: spread_occ(2 * n + 2, c), 0)

    own_size = sizes[row]
    owner, function = function_of(iota((W, 1), 0))
    eye = iota((W, W), 1) == owner * SUB + function
    ri_block = iota((1, W), 1) // PB

    def keep_of(e):
        keep = jnp.zeros((1, W), jnp.float32)
        for q in range(W // PB):
            value = ri[e, row, (W // PB) * col + q].astype(jnp.float32)
            keep = jnp.where(ri_block == q, value, keep)
        return jnp.where(eye, keep, 0.0).astype(bf)

    def turn(p, diag):
        lane = iota((1, PIECE), 1) + p % 2 * PIECE
        partner = sizes[wrap(row + p // 2 - 1, NB)]
        fill = jnp.where(((lane >> 5) < own_size) & ((lane & 31) < partner), 1.0, 0.0)
        right[p, 0:W, :] = (dot(diag, ints[p % 3], NT) * fill).astype(bf)

    diag = None
    for p in range(NPIECE):
        if p % 2 == 0:
            diag = keep_of(p // 2)
        loads[p].wait()
        turn(p, diag)
        if p + 3 < NPIECE:
            loads[p + 3].start()
    pl.semaphore_wait(barrier, 8)

    def meet_signal(n, targets):
        for target in targets:
            pl.semaphore_signal(meet.at[n], inc=1, device_id=target, device_id_type=MESH)

    def meet_wait(n):
        pl.semaphore_wait(meet.at[n], 2)

    meet_signal(0, y_dev)

    def gather_copies(view, far_view, sems, targets):
        send, recv, on_send, on_recv = sems
        own, onward = {}, {}
        for way in (0, 1):
            for q in range(NPIECE):
                own[way, q] = remote(
                    view(q, 1, 0, 0, W), view(q, 1, 1 + way, 0, W), send.at[way, q], recv.at[way, q], targets[way]
                )
            for late in (0, 1):
                part = 2 * late + way
                for order in range(ND):
                    onward[way, late, order] = remote(
                        view(2 * order, 2, 1 + way, BASE[part], PART_ROWS[part]),
                        far_view(2 * order, 2, part),
                        on_send.at[way, late, order],
                        on_recv.at[way, late, order],
                        targets[way],
                    )
        return own, onward

    def right_view(q, n, slot, first, rows):
        return right.at[pl.ds(2 * bands[q // 2] + q % 2, n), pl.ds(QOFF[slot] + first, rows), :]

    def right_far(q, n, part):
        return right.at[pl.ds(2 * bands[q // 2], n), pl.ds(QFAR[part], PART_ROWS[part]), :]

    def left_view(p, n, slot, first, rows):
        return left.at[pl.ds(p, n), slot, pl.ds(first, rows), :]

    def left_far(p, n, part):
        return left_view(p, n, 3, BASE[part], PART_ROWS[part])

    r_own, r_on = gather_copies(right_view, right_far, (r_send, r_recv, rf_send, rf_recv), y_dev)
    l_own, l_on = gather_copies(left_view, left_far, (l_send, l_recv, lf_send, lf_recv), z_dev)
    for p in range(NPIECE):
        for way in (0, 1):
            r_own[way, p].start()

    halos = {}
    for n, (band, target) in enumerate(((1, other), (near, other), (1, far_halo), (far, far_halo))):
        halos[n] = remote(mixed.at[band], halo.at[n], h_send.at[n], h_recv.at[n], target)

    def mix(dm, pairs):
        def body(g, _):
            h, start = g // 2, pl.multiple_of(lax.rem(g, 2) * LANES, LANES)
            total = None
            for e, f in pairs:
                term = dot(right[2 * e + h, 0:W, pl.ds(start, LANES)], occ_mat[ND * e + f - 1])
                total = term if total is None else total + term
            mixed[dm, :, pl.ds(pl.multiple_of(g * LANES, LANES), LANES)] = total.astype(bf)
            return 0

        lax.fori_loop(0, BLK * BLK // LANES, body, 0)

    mix(1, ((0, 2), (1, 1), (2, 0)))
    halos[0].start()
    halos[2].start()
    lax.fori_loop(0, 4, lambda n, c: spread_occ(2 * n + 1, c), 0)
    mix(near, ((near // 2, near + 1 - near // 2), (near // 2 + 1, near - near // 2)))
    halos[1].start()

    match[...] = jnp.where(iota(match.shape, 0) == (iota(match.shape, 1) & 31), 1.0, 0.0)
    repeat = ((iota((BLK, BLK * BLK), 1) >> 5) == iota((BLK, BLK * BLK), 0)).astype(bf)

    def spread_vir(g):
        block = (vir[row, g].astype(jnp.float32) * vir_pat[g, row].astype(jnp.float32)).astype(bf)
        tall[...] = dot(block, repeat, (((0,), (0,)), ((), ())))

        def body(a, _):
            rows = tall[pl.ds(a, 1), :] * match[...]
            vir_mat[g, pl.ds(pl.multiple_of(a * BLK, BLK), BLK), :] = rows.astype(bf)
            return 0

        lax.fori_loop(0, BLK, body, 0)

    def contract(order, terms):
        for h in (0, 1):
            total = None
            for ref, index, g in terms:
                term = dot(ref[index], vir_mat[g, :, PIECE * h : PIECE * (h + 1)])
                total = term if total is None else total + term
            left[2 * order + h, 0] = total.astype(bf)
            for way in (0, 1):
                l_own[way, 2 * order + h].start()

    meet_wait(0)
    meet_signal(1, z_dev)
    spread_vir(1)
    spread_vir(near)
    halos[0].wait_recv()
    contract(0, ((mixed, near, 1), (halo, 0, near)))
    mix(far, ((far // 2, far + 1 - far // 2), (far // 2 + 1, far - far // 2)))
    halos[3].start()
    spread_vir(far)
    halos[2].wait_recv()
    contract(1, ((mixed, far, 1), (halo, 2, far)))
    halos[1].wait_recv()
    halos[3].wait_recv()
    contract(2, ((mixed, 1, 1), (halo, 1, near), (halo, 3, far)))

    owner, function = function_of(iota((W, 1), 0))
    one_hot[...] = jnp.where(iota((W, 8 * 128), 1) == owner * 128 + function, 1.0, 0.0).astype(bf)
    lane = iota((1, NX * 128), 1)
    inside = lane & 127
    late = (inside >= SUB).astype(jnp.int32)
    column = (4 * late + (lane >> 7)) * SUB + inside - SUB * late
    place[...] = jnp.where((inside < 2 * SUB) & (iota(place.shape, 0) == column), 1.0, 0.0).astype(bf)
    source = iota((NX * SLOT, 1), 0)
    part = (source >> 4) & 3
    inside = source & 15
    target = (source >> 6) * SUB + PARTS[0] * part + inside
    real = inside < jnp.where(part == 3, PARTS[3], PARTS[0])
    for i, (n, yy) in enumerate(PLACES):
        lane = iota(choose.shape[1:], 1) + (LANES * n - NX * SUB * yy)
        choose[i] = jnp.where(real & (lane == target), 1.0, 0.0).astype(bf)
    for p in range(NPIECE):
        right[p, 1200:1280, :] = jnp.zeros((80, PIECE), bf)
        right[p, 1472:1536, :] = jnp.zeros((64, PIECE), bf)
        right[p, 1744:1792, :] = jnp.zeros((48, PIECE), bf)
    acc[W:, :] = jnp.zeros((acc.shape[0] - W, acc.shape[1]), jnp.float32)
    near_acc[2 * W :, :] = jnp.zeros((near_acc.shape[0] - 2 * W, near_acc.shape[1]), jnp.float32)

    def product(slot, count, first, lanes, total, rows=(0, W), orders=(0, 1, 2), add=False, into=0):
        p_rows = pl.ds(rows[0], rows[1] - rows[0])
        out_rows = p_rows if count == 1 else pl.ds(0, W * count)

        def left_rows(piece):
            if count == 1:
                return left[piece, slot, p_rows, :]
            return left[piece, slot : slot + count].reshape(count * W, PIECE)

        def body(n, _):
            lane = pl.ds(pl.multiple_of(into + n * LANES, LANES), LANES)
            q_rows = pl.ds(pl.multiple_of(first + n * LANES, LANES), LANES)
            value = total[out_rows, lane] if add else None
            for order in orders:
                for h in (0, 1):
                    term = dot(left_rows(2 * order + h), right[2 * bands[order] + h, q_rows, :], NT)
                    value = term if value is None else value + term
            total[out_rows, lane] = value
            return 0

        lax.fori_loop(0, lanes // LANES, body, 0)

    def split(n, which, total, row=0, lane=0):
        _, some, _, lanes, _ = GROUPS[n]
        for s in range(8):
            for i, part in enumerate(some):
                first = row + BASE[part] + s * PARTS[part]
                parts[n][s % 2, s // 2, which, TILE * i : TILE * i + TILE] = total[first : first + TILE, lane : lane + lanes].astype(bf)

    core_copy, hop_copy = {}, {}

    def core_start(n):
        core_copy[n] = remote(parts[n].at[1 - k], cores[n], c_send.at[n], c_recv.at[n], other)
        core_copy[n].start()

    def halves(n):
        half = TILE * len(GROUPS[n][1]) // 2
        return pl.ds(0, half), pl.ds(half, half)

    def hop(n, way, m, src):
        hop_copy[n, way, m] = remote(
            src, hops[n].at[way, m], x_send.at[n, way, m], x_recv.at[n, way, m], x_dev[way]
        )
        hop_copy[n, way, m].start()

    def stage1(n):
        ref, extra = parts[n], cores[n]
        low, high = halves(n)
        core_copy[n].wait_recv()
        mine = ref.at[k]

        def join(b):
            mine[b] = (mine[b].astype(jnp.float32) + extra[b].astype(jnp.float32)).astype(bf)

        join(far_x)
        hop(n, 0, 0, mine.at[far_x, :, low, :])
        hop(n, 1, 0, mine.at[far_x, :, high, :])
        join(up_x)
        hop(n, 0, 1, mine.at[up_x, :, high, :])
        join(down_x)
        hop(n, 1, 1, mine.at[down_x, :, low, :])
        join(x)

    def stage2(n):
        mine = parts[n].at[k]
        low, high = halves(n)
        for way, b, rows in ((0, up_x, low), (1, down_x, high)):
            hop_copy[n, way, 0].wait_recv()
            mine[b, :, rows, :] = (
                mine[b, :, rows, :].astype(jnp.float32) + hops[n][way, 0].astype(jnp.float32)
            ).astype(bf)
            hop(n, way, 2, mine.at[b, :, rows, :])

    def stage3(n):
        slots, some, first, _, q_pieces = GROUPS[n]
        mine = parts[n].at[k]
        low, high = halves(n)
        half = TILE * len(some) // 2
        for way in (0, 1):
            for m in (1, 2):
                hop_copy[n, way, m].wait_recv()
        for rows, one, two, start in ((low, 2, 1, 0), (high, 1, 2, half)):
            total = (
                mine[x, :, rows, :].astype(jnp.float32)
                + hops[n][0, one].astype(jnp.float32)
                + hops[n][1, two].astype(jnp.float32)
            )
            start += TILE * some[0]
            for i, slot in enumerate(slots):
                for q, lane, into, width in q_pieces:
                    there = wrap(y + (0, -1, 1, 2)[q])
                    block = total[i, :, lane - first : lane - first + width].astype(bf)
                    rows_in = pl.ds(SLOT * slot + start, half)
                    fin[lax.rem(there, 2), there // 2, rows_in, into : into + width] = block

    exchange = {}

    own_pair = y // 2

    def exchange_start(n, first, count, pairs, some=None):
        rows = pl.ds(first, count)
        packed = None
        for yy in (0, 1):
            chunks = [fin[yy, pair, rows, :] for pair in pairs]
            term = dot(chunks[0] if len(chunks) == 1 else jnp.concatenate(chunks, axis=0), one_hot[...])
            packed = term if packed is None else packed + pltpu.roll(term, SUB, 1)
        packed = packed.astype(bf)
        for i, pair in enumerate(pairs):
            for s in range(8):
                target = NX * (s // 2) + 2 * (s % 2) + pair
                msgs[target, rows, :] = packed[count * i : count * (i + 1), 128 * s : 128 * s + 128]

        def copy(m):
            target = NX * wrap(y + m // NX) + wrap(z + lax.rem(m, NX))
            return remote(
                msgs.at[target, rows, :], got.at[col, rows, :], a_send.at[n, m - 1], a_recv.at[n, m - 1], (row, target)
            )

        exchange[n] = copy

        for m in FAR_FIRST:
            if some is None:
                copy(m).start()
            else:
                pl.when(lax.rem(z + m, 2) == some)(copy(m).start)

    def exchange_wait(n, what):
        for m in FAR_FIRST:
            if what == "recv":
                exchange[n](m).wait_recv()
            else:
                exchange[n](m).wait_send()

    def arrive(order, own, onward):
        for way in (0, 1):
            own[way, 2 * order].wait_recv()
            own[way, 2 * order + 1].wait_recv()
            onward[way, 0, order].start()

    def pass_late(onward):
        for order in range(ND):
            for way in (0, 1):
                onward[way, 1, order].start()

    def far_arrive(onward, late, orders=(0, 1, 2)):
        for order in orders:
            for way in (0, 1):
                onward[way, late, order].wait_recv()

    for order in range(ND):
        arrive(order, r_own, r_on)
        if order == ND - 1:
            pass_late(r_on)
        product(0, 1, 0, 1280, acc, orders=(order,), add=order > 0)
    split(0, 0, acc)
    core_start(0)
    meet_wait(1)
    meet_signal(2, z_dev)
    for order in range(ND):
        arrive(order, l_own, l_on)
        if order == ND - 1:
            pass_late(l_on)
        product(1, 2, 0, 1280, near_acc, orders=(order,), add=order > 0)
        if order == 0:
            stage1(0)
        if order == 1:
            stage2(0)
    split(1, 0, near_acc)
    core_start(1)
    split(2, 0, near_acc, W)
    core_start(2)
    meet_wait(2)
    stage1(1)
    far_arrive(r_on, 0)
    product(1, 2, 1280, 256, near_acc)
    product(0, 1, 1280, 256, near_acc, into=256)
    split(3, 0, near_acc, 0, 256)
    split(3, 1, near_acc)
    split(3, 2, near_acc, W)
    core_start(3)
    stage1(2)
    stage2(1)
    stage3(0)
    stage1(3)
    stage2(2)
    early, late = (0, BASE[2]), (BASE[2], W)
    far_arrive(l_on, 0)
    product(3, 1, 0, 1536, acc, early)
    stage3(1)
    stage2(3)
    far_arrive(r_on, 1)
    product(3, 1, 1536, 256, acc, early, into=1536)
    split(5, 0, acc)
    core_start(5)
    product(1, 2, 1536, 256, near_acc)
    product(0, 1, 1536, 256, near_acc, into=256)
    split(4, 0, near_acc, 0, 256)
    split(4, 1, near_acc)
    split(4, 2, near_acc, W)
    core_start(4)
    stage1(5)
    stage1(4)
    stage3(2)
    far_arrive(l_on, 1, (0,))
    product(3, 1, 0, 1792, acc, late, (0,))
    stage2(5)
    stage3(3)
    far_arrive(l_on, 1, (1,))
    product(3, 1, 0, 1792, acc, late, (1,), True)
    stage2(4)
    exchange_start(0, 0, 3 * SLOT, (own_pair,), own_pair)
    far_arrive(l_on, 1, (2,))
    product(3, 1, 0, 1792, acc, late, (2,), True)
    split(6, 0, acc)
    core_start(6)
    stage1(6)
    stage3(5)
    stage3(4)
    exchange_start(0, 0, 3 * SLOT, (1 - own_pair,), 1 - own_pair)
    stage2(6)
    stage3(6)
    exchange_start(1, 3 * SLOT, SLOT, (0, 1))
    got[col] = msgs[col]

    for n in (0, 1):
        exchange_wait(n, "recv")
    slot_of = {0: 0, 3: 1, 1: 2, 2: 3}
    for copy in halos.values():
        copy.wait_send()
    wide = mixed.at[0]
    for yy in range(NX):
        rows = [
            jnp.concatenate([got[NX * yy + src, pl.ds(SLOT * slot_of[(zz - src) % NX], SLOT)] for src in range(NX)], axis=1)
            for zz in range(NX)
        ]
        wide[:, 256 * yy : 256 * yy + 256] = dot(place[...], jnp.concatenate(rows, axis=0), NT).astype(bf)
    for n in range(4):
        width = min(LANES, 800 - LANES * n)
        total = None
        for i, (tile, yy) in enumerate(PLACES):
            if tile == n:
                term = dot(wide[:, 256 * yy : 256 * yy + 256], choose[i, :, 0:width])
                total = term if total is None else total + term
        out[:, LANES * n : LANES * n + width] = total.astype(bf)

    for copies in (r_own, r_on, l_own, l_on, core_copy, hop_copy):
        for copy in copies.values():
            copy.wait_send()
    for n in (0, 1):
        exchange_wait(n, "send")


def local(integrals, block_sizes, int_pattern, occ_density, occ_pattern, vir_density, vir_pattern):
    ints = integrals.reshape(ND, BLK * BLK, W)
    bf = jnp.bfloat16
    vmem = pl.BlockSpec(memory_space=pltpu.VMEM)
    smem = pl.BlockSpec(memory_space=pltpu.SMEM)
    dma = pltpu.SemaphoreType.DMA
    shapes = [(len(slots), TILE * len(some), lanes) for slots, some, _, lanes, _ in GROUPS]
    scratch = [
        pltpu.VMEM((3, PIECE, W), bf),
        pltpu.VMEM((NPIECE, QROWS, PIECE), bf),
        pltpu.VMEM((NPIECE, NX, W, PIECE), bf),
        pltpu.VMEM((ND, W, BLK * BLK), bf),
        pltpu.VMEM((4, W, BLK * BLK), bf),
        pltpu.VMEM((ND * ND - 2, LANES, LANES), bf),
        pltpu.VMEM((ND, BLK * BLK, BLK * BLK), bf),
        pltpu.VMEM((BLK, BLK * BLK), jnp.float32),
        pltpu.VMEM((BLK, BLK * BLK), jnp.float32),
        pltpu.VMEM((416, QROWS), jnp.float32),
        pltpu.VMEM((2 * W + 16, 1280), jnp.float32),
        pltpu.VMEM((2, 2, NX * SLOT, W), bf),
        pltpu.VMEM((W, 8 * 128), bf),
        pltpu.VMEM((W, NX * 128), bf),
        pltpu.VMEM((len(PLACES), LANES, LANES), bf),
        pltpu.VMEM((NX * NX, NX * SLOT, 128), bf),
        pltpu.VMEM((NX * NX, NX * SLOT, 128), bf),
        *[pltpu.VMEM((2, NX, n, rows, lanes), bf) for n, rows, lanes in shapes],
        *[pltpu.VMEM((NX, n, rows, lanes), bf) for n, rows, lanes in shapes],
        *[pltpu.VMEM((2, 3, n, rows // 2, lanes), bf) for n, rows, lanes in shapes],
        dma((NPIECE,)),
        *[dma((2, NPIECE)), dma((2, NPIECE)), dma((2, 2, ND)), dma((2, 2, ND))] * 2,
        dma((4,)), dma((4,)),
        dma((NG,)), dma((NG,)),
        dma((NG, 2, 3)), dma((NG, 2, 3)),
        dma((2, NX * NX - 1)), dma((2, NX * NX - 1)),
        pltpu.SemaphoreType.REGULAR((3,)),
    ]
    response = pl.pallas_call(
        kernel,
        out_shape=jax.ShapeDtypeStruct((W, 800), bf),
        in_specs=[smem, smem, smem, smem, pl.BlockSpec(memory_space=pl.ANY), vmem, vmem],
        out_specs=vmem,
        scratch_shapes=scratch,
        compiler_params=pltpu.CompilerParams(
            collective_id=0, has_side_effects=True, vmem_limit_bytes=64 * 1024 * 1024
        ),
    )(block_sizes, int_pattern.transpose(1, 0, 2), occ_pattern.T, vir_pattern.T, ints, occ_density, vir_density)
    return response.astype(jnp.float32).T


def solution(mesh):
    return jax.shard_map(
        local,
        mesh=mesh,
        in_specs=(P("row", None, None, None, "col"), P(), P(), P(), P(), P(), P()),
        out_specs=P("row", "col"),
        check_vma=False,
    )
```
